256 devices in a mesh: dom: 64 (over z, y, core), feat: 4 (over x).
Axes of the slice: x: 4, y: 4, z: 8, core: 2. Of those that a mesh axis runs over, the one named last changes fastest.
Arguments:
- quantized: bfloat16 [128, 524288], P('feat', 'dom'), may hold values from -4 to 4
- node_scale: float32 [524288], P('dom'), may hold values from 0.25 to 4
- send_rows: int32 [64, 64, 192], P('dom'), may hold values from 0 to 8191
- send_count: int32 [64, 64], P('dom'), may hold values from 1 to 192, 9216 in all within a row
- tile_cols: int32 [64, 64, 4], P('dom'), may hold values from 0 to 159, as said below
- edge_tiles: int32 [4096, 4, 128, 128], P('dom'), may hold values 0 or 1
- self_weight: bfloat16 [128, 256], P('feat'), may hold values from -0.5 to 0.5
- neighbor_weight: bfloat16 [128, 256], P('feat'), may hold values from -4 to 4
- hidden_bias: float32 [256], P('feat'), may hold values from -3 to 3
- upstream: bfloat16 [256, 524288], P('feat', 'dom'), may hold values from -6 to 6
Outputs:
- hidden: bfloat16 [256, 524288], P('feat', 'dom')
- grad_features: float32 [128, 524288], P('feat', 'dom')
- grad_self: float32 [128, 256], P('feat')
- grad_neighbor: float32 [128, 256], P('feat')
- grad_bias: float32 [256], P('feat')
The draws below stay inside these ranges and needn't reach their ends.
Inputs may be any that keep to these rules, and one draw needn't show every extreme that they name: `send_rows`: indices of nodes within the sending partition. Each row of send_count sums to 9216 and its largest entry is exactly 192. `tile_cols`: in each partition every one of the 160 column tiles is named by some row tile.
All inputs are finite; a program needn't handle non-finite values. No bound on the sum of `edge_tiles` on one device may be relied on, other than what follows from the above.
Results may differ from the reference program's by a relative error of at most 0.008.
Values may be sent and summed in bfloat16 or wider, within the bound.
No kernel may reach another device: no remote copies, remote signals or barrier semaphores. Data moves between devices by JAX's collectives and lax.ppermute only.
A program may use at most 128 MiB of HBM per device.

```python
import math
import jax
import jax.numpy as jnp
import numpy as np
from jax import lax

F_IN = 128
H = 256
TILE = 128
K = 4
TILES_DEV = 64
HALO_DEV = 12288
NODE_DEV = 8192
NODES = 524288
SLOT = 192
N_DOM = 64


def draw_tile_cols(key, part):
    key = jax.random.fold_in(key, 7)
    device_keys = jax.random.split(key, N_DOM)
    orders = jax.vmap(lambda subkey: jax.random.permutation(subkey, TILES_DEV * K))(device_keys)
    return (orders % (TILES_DEV + HALO_DEV // TILE)).reshape(N_DOM, TILES_DEV, K).astype(jnp.int32)


def with_ends(array, own_key, low, largest):
    longest = array.shape.index(max(array.shape))
    spots = []
    for shift in (0, 1):
        where = [jax.random.randint(jax.random.fold_in(own_key, axis), (), 0, length) for axis, length in enumerate(array.shape)]
        where[longest] = (where[longest] + shift) % array.shape[longest]
        spots.append(tuple(where))
    return array.at[spots[0]].set(low).at[spots[1]].set(largest)


def level_of(key, shape, cuts, least, high):
    gain = 1.0
    for axis_at, blocks in cuts:
        steps = jax.random.uniform(jax.random.fold_in(jax.random.fold_in(key, 6), axis_at), (blocks,), jnp.float32, least / len(cuts), high / len(cuts))
        gain = gain * jnp.repeat(jnp.exp(steps), shape[axis_at] // blocks).reshape((-1,) + (1,) * (len(shape) - 1 - axis_at))
    return gain


def profile(number_of, total, limit, lean):
    weights = [(1 << 20) // math.isqrt(standing ** lean) + 1 for standing in range(2, number_of + 1)]
    rest, counts = total - limit - (number_of - 1), [1] * (number_of - 1)
    while rest > 0:
        candidates = [i for i in range(number_of - 1) if counts[i] < limit]
        whole, left = sum([weights[i] for i in candidates]), rest
        for i in candidates:
            more = min(limit - counts[i], max(1, left * weights[i] // whole), rest)
            counts[i] = counts[i] + more
            rest = rest - more
    return np.array([limit] + counts)


def uneven_parts(key, count, total, most, skew):
    if count == 2:
        one = jax.random.randint(key, (), max(1, total - most), min(most, total - 1) + 1)
        return jnp.stack([one, total - one])
    sizes = jnp.asarray(profile(count, total, most, skew), jnp.int32)
    pairs = (count - 1) // 2
    donor, taker = sizes[1:1 + 2 * pairs:2], sizes[2:2 + 2 * pairs:2]
    margin = jnp.minimum(donor - 1, most - taker)
    shifted = jax.random.randint(jax.random.fold_in(key, 1), (pairs,), 0, 1 << 20) % (margin + 1)
    sizes = sizes.at[1:1 + 2 * pairs:2].set(donor - shifted).at[2:2 + 2 * pairs:2].set(taker + shifted)
    return sizes[jax.random.permutation(jax.random.fold_in(key, 2), count)]


def gaussian(key, extent, width, bound, cuts=(), kind=jnp.bfloat16):
    values = jax.random.normal(key, extent, jnp.float32) * width
    if len(cuts) > 0:
        values = level_of(key, extent, cuts, -0.22, 0.18) * values
    return jnp.clip(values, min=-bound, max=bound).astype(kind)


def setup_inputs(seed: int = 0) -> dict:
    seeds = jax.random.split(jax.random.key(seed), 11)
    return {
        "quantized": gaussian(seeds[0], (F_IN, NODES), 1.0, 4.0, ((0, 4), (1, 64))),
        "node_scale": jnp.clip(jnp.exp(math.log(4.0) - 2.7725887 * jax.random.uniform(seeds[1], (NODES,), jnp.float32) ** level_of(seeds[1], (NODES,), ((0, 64),), -0.2, 0.2)), 0.25, 4.0),
        "send_rows": with_ends(jax.random.randint(seeds[2], (N_DOM, N_DOM, SLOT), 0, NODE_DEV), jax.random.fold_in(seeds[2], 1), 0, NODE_DEV - 1).astype(jnp.int32),
        "send_count": jax.vmap(lambda own: uneven_parts(own, N_DOM, 3 * HALO_DEV // 4, SLOT, 2))(jax.random.split(seeds[3], N_DOM)).reshape((N_DOM, N_DOM)).astype(jnp.int32),
        "tile_cols": draw_tile_cols(jax.random.fold_in(seeds[10], 71), 0),
        "edge_tiles": with_ends((jax.random.randint(seeds[5], (N_DOM * TILES_DEV, K, TILE, TILE), 0, 8) < 1).astype(jnp.int32), jax.random.fold_in(seeds[5], 1), 0, 1),
        "self_weight": gaussian(seeds[6], (F_IN, H), F_IN ** -0.5, 0.5, ((0, 4),)),
        "neighbor_weight": gaussian(seeds[7], (F_IN, H), (max(F_IN // 64, 1)) ** -0.5, 4.0, ((0, 4),)),
        "hidden_bias": gaussian(seeds[8], (H,), 0.5, 3.0, ((0, 4),), jnp.float32),
        "upstream": gaussian(seeds[9], (H, NODES), 1.0, 6.0, ((0, 4), (1, 64))),
    }


def reference(quantized, node_scale, send_rows, send_count, tile_cols, edge_tiles, self_weight, neighbor_weight, hidden_bias, upstream):
    peer_count = N_DOM
    node_count = TILES_DEV * TILE
    slot_count = HALO_DEV // N_DOM
    col_count = TILES_DEV + HALO_DEV // TILE
    features = (quantized.astype(jnp.float32) * node_scale[None, :]).astype(jnp.bfloat16)
    parts = features.reshape(F_IN, peer_count, node_count).transpose(1, 0, 2)
    slot_index = lax.broadcasted_iota(jnp.int32, (peer_count, peer_count, slot_count), 2)
    live_slots = (slot_index < send_count[:, :, None]).astype(jnp.bfloat16)
    flat_rows = send_rows.reshape(peer_count, peer_count * slot_count)
    outgoing = jax.vmap(lambda block, chosen: jnp.take(block, chosen, axis=1))(parts, flat_rows)
    outgoing = outgoing.reshape(peer_count, F_IN, peer_count, slot_count) * live_slots[:, None, :, :]
    incoming = outgoing.transpose(2, 1, 0, 3).reshape(peer_count, F_IN, peer_count * slot_count)
    mask_parts = edge_tiles.reshape(peer_count, TILES_DEV, K, TILE, TILE)
    degree = jnp.sum(mask_parts, axis=(2, 4)).reshape(peer_count, node_count).astype(jnp.float32)

    def aggregate_one(inputs):
        own_rows, halo_rows, tile_index, mask_tiles = inputs
        joined = jnp.concatenate([own_rows, halo_rows], axis=1).reshape(F_IN, col_count, TILE)
        picked = jnp.take(joined, tile_index, axis=1).astype(jnp.float32)
        summed = jnp.einsum("ftkj,tkij->fti", picked, mask_tiles.astype(jnp.float32))
        return summed.reshape(F_IN, node_count)

    neighbor_sum = lax.map(aggregate_one, (parts, incoming, tile_cols, mask_parts))
    aggregate_parts = ((neighbor_sum + parts.astype(jnp.float32)) / (degree[:, None, :] + 1.0)).astype(jnp.bfloat16)
    aggregate = aggregate_parts.transpose(1, 0, 2).reshape(F_IN, peer_count * node_count)
    preact = jnp.dot(self_weight.T, features, preferred_element_type=jnp.float32)
    preact = preact + jnp.dot(neighbor_weight.T, aggregate, preferred_element_type=jnp.float32) + hidden_bias[:, None]
    sigmoid_z = jax.nn.sigmoid(preact)
    hidden = (preact * sigmoid_z).astype(jnp.bfloat16)
    slope = (upstream.astype(jnp.float32) * sigmoid_z * (1.0 + preact * (1.0 - sigmoid_z))).astype(jnp.bfloat16)
    grad_self = jnp.dot(features, slope.T, preferred_element_type=jnp.float32)
    grad_neighbor = jnp.dot(aggregate, slope.T, preferred_element_type=jnp.float32)
    grad_bias = jnp.sum(slope.astype(jnp.float32), axis=1)
    mean_grad = jnp.dot(neighbor_weight, slope, preferred_element_type=jnp.float32) / (degree.reshape(-1) + 1.0)[None, :]
    self_grad = jnp.dot(self_weight, slope, preferred_element_type=jnp.float32)
    mean_grad_b = mean_grad.astype(jnp.bfloat16)
    mean_parts = mean_grad_b.reshape(F_IN, peer_count, node_count).transpose(1, 0, 2)

    def spread_one(inputs):
        piece, tile_index, mask_tiles = inputs
        contrib = jnp.einsum("fti,tkij->tkfj", piece.reshape(F_IN, TILES_DEV, TILE).astype(jnp.float32), mask_tiles.astype(jnp.float32))
        summed = jax.ops.segment_sum(contrib.reshape(TILES_DEV * K, F_IN, TILE), tile_index.reshape(-1), num_segments=col_count)
        return summed.transpose(1, 0, 2).reshape(F_IN, col_count * TILE)

    joined_grad = lax.map(spread_one, (mean_parts, tile_cols, mask_parts))
    local_grad = joined_grad[:, :, :node_count]
    halo_grad = joined_grad[:, :, node_count:].reshape(peer_count, F_IN, peer_count, slot_count)
    returning = halo_grad.transpose(2, 1, 0, 3).reshape(peer_count, F_IN, peer_count * slot_count)
    returning = returning * live_slots.reshape(peer_count, 1, peer_count * slot_count).astype(jnp.float32)

    def place_one(values, chosen):
        return jnp.zeros((F_IN, node_count), jnp.float32).at[:, chosen].add(values)

    returned = jax.vmap(place_one)(returning, flat_rows)
    gathered = (local_grad + returned).transpose(1, 0, 2).reshape(F_IN, peer_count * node_count)
    grad_features = self_grad + mean_grad + gathered
    return hidden, grad_features, grad_self, grad_neighbor, grad_bias
```

```python
import functools

import jax
import jax.numpy as jnp
from jax import lax
from jax.experimental import pallas as pl
from jax.experimental.pallas import tpu as pltpu
from jax.sharding import PartitionSpec as P

BF = jnp.bfloat16
F32 = jnp.float32
VMEM = pl.BlockSpec(memory_space=pltpu.VMEM)
SMEM = pl.BlockSpec(memory_space=pltpu.SMEM)
LANES = 128
CHUNK = 512
GROUP = 4


def params(limit=48 << 20, **kw):
    return pltpu.CompilerParams(vmem_limit_bytes=limit, **kw)


def cost(flops, nbytes):
    return pl.CostEstimate(flops=int(flops), bytes_accessed=int(nbytes), transcendentals=0)


def low_half(shape):
    return lax.broadcasted_iota(jnp.int32, shape, len(shape) - 1) < LANES // 2


def split_rest(tile):
    half = tile.shape[0] // 2
    a, b = tile[:half], tile[half:]
    low = low_half(a.shape)
    even = jnp.where(low, a, pltpu.roll(b, LANES // 2, 1))
    odd = jnp.where(low, pltpu.roll(a, LANES // 2, 1), b)
    return even, odd


def join_rest(even, odd):
    low = low_half(even.shape)
    a = jnp.where(low, even, pltpu.roll(odd, LANES // 2, 1))
    b = jnp.where(low, pltpu.roll(even, LANES // 2, 1), odd)
    return jnp.concatenate([a, b], axis=0)


def one_hot_rows(lo):
    rows = lax.broadcasted_iota(jnp.int32, (CHUNK, lo.shape[1]), 0)
    return jnp.where(rows == lo, 1.0, 0.0).astype(BF)


def gather_kernel(me_ref, quantized, scale, idx, feat_tiles, wire, *rest):
    blocks, (folded,) = rest[:4], rest[4:]
    feature_count, node_count = quantized.shape
    fold = node_count // CHUNK
    width = node_count // 4
    me = me_ref[0]
    for c in range(fold):
        at = pl.ds(c * CHUNK, CHUNK)
        part = (quantized[:, at].astype(F32) * scale[:, at]).astype(BF)
        folded[c * feature_count : (c + 1) * feature_count, :] = part
        for t in range(CHUNK // LANES):
            feat_tiles[c * (CHUNK // LANES) + t] = part[:, t * LANES : (t + 1) * LANES]
    per_block = width // CHUNK
    for s in range(4):
        first = lax.rem(me + s, 4) * per_block
        for c in range(per_block):
            src = pl.ds(pl.multiple_of((first + c) * feature_count, feature_count), feature_count)
            blocks[s][:, c * CHUNK : (c + 1) * CHUNK] = folded[src, :]

    def pick(base):
        rows = [idx[pl.ds(base + t, 1), :] for t in range(4)]
        row = jnp.concatenate(rows, axis=1)
        hi, lo = row >> 9, row & (CHUNK - 1)
        out = jnp.dot(folded[...], one_hot_rows(lo), preferred_element_type=F32)
        total = jnp.zeros((feature_count, row.shape[1]), F32)
        for c in range(fold):
            total = total + jnp.where(hi == c, out[c * feature_count : (c + 1) * feature_count], 0.0)
        return [total[:, t * LANES : (t + 1) * LANES] for t in range(4)]

    @pl.loop(0, 16)
    def _(g):
        tiles = pick(g * 4)
        for t in range(4):
            wire[g * 4 + t, 0:feature_count, :] = tiles[t].astype(BF)

    @pl.loop(0, 8)
    def _(g):
        tiles = pick(64 + g * 4)
        for t in range(4):
            even, odd = split_rest(tiles[t])
            wire[(g * 4 + t) * 2, feature_count:48, :] = even.astype(BF)
            wire[(g * 4 + t) * 2 + 1, feature_count:48, :] = odd.astype(BF)


def gather(me, quantized, scale, idx):
    rows, nodes = quantized.shape
    return pl.pallas_call(
        gather_kernel,
        out_shape=[
            jax.ShapeDtypeStruct((nodes // LANES, rows, LANES), BF),
            jax.ShapeDtypeStruct((64, 48, LANES), BF),
        ]
        + [jax.ShapeDtypeStruct((rows, nodes // 4), BF)] * 4,
        in_specs=[SMEM, VMEM, VMEM, VMEM],
        out_specs=[VMEM] * 6,
        scratch_shapes=[pltpu.VMEM((rows * nodes // CHUNK, CHUNK), BF)],
        compiler_params=params(),
        cost_estimate=cost(6.4e9, 4 << 20),
        name="gather_rows",
    )(me, quantized, scale, idx)


def mask_kernel(edges, mask, degree):
    ones = jnp.ones((8, LANES * 4), BF)
    parts = []
    for r in range(GROUP):
        m = edges[r].astype(F32).astype(BF)
        mask[r] = m
        flat = jnp.concatenate([m[k] for k in range(4)], axis=1)
        parts.append(
            lax.dot_general(ones, flat, (((1,), (1,)), ((), ())), preferred_element_type=F32)
        )
    degree[0] = jnp.concatenate(parts, axis=1)


def masks(edges):
    steps = edges.shape[0] // GROUP
    return pl.pallas_call(
        mask_kernel,
        grid=(steps,),
        out_shape=[
            jax.ShapeDtypeStruct(edges.shape, BF),
            jax.ShapeDtypeStruct((steps, 8, GROUP * LANES), F32),
        ],
        in_specs=[pl.BlockSpec((GROUP, 4, LANES, LANES), lambda i: (i, 0, 0, 0))],
        out_specs=[
            pl.BlockSpec((GROUP, 4, LANES, LANES), lambda i: (i, 0, 0, 0)),
            pl.BlockSpec((1, 8, GROUP * LANES), lambda i: (i, 0, 0)),
        ],
        compiler_params=params(),
        cost_estimate=cost(1e9, 24 << 20),
        name="mask_degree",
    )(edges)


def join_kernel(feat_tiles, wire, joined):
    local = feat_tiles.shape[0]
    joined[0:local] = feat_tiles[...]

    @pl.loop(0, 32)
    def _(q):
        even, odd = wire[2 * q], wire[2 * q + 1]
        joined[local + 3 * q] = even[0:32]
        joined[local + 3 * q + 2] = odd[0:32]
        joined[local + 3 * q + 1] = join_rest(even[32:48].astype(F32), odd[32:48].astype(F32)).astype(BF)


def join(feat_tiles, wire):
    count = feat_tiles.shape[0] + 96
    return pl.pallas_call(
        join_kernel,
        out_shape=jax.ShapeDtypeStruct((count,) + feat_tiles.shape[1:], BF),
        in_specs=[VMEM, VMEM],
        out_specs=VMEM,
        compiler_params=params(),
        cost_estimate=cost(1e6, 3 << 20),
        name="join_tiles",
    )(feat_tiles, wire)


def aggregate_kernel(shift, me_ref, cols, joined, mask, degree, out):
    step = pl.program_id(0)
    group = lax.rem(me_ref[0] + shift, 4) * 4 + step
    for r in range(GROUP):
        row = group * GROUP + r
        picked = jnp.concatenate([joined[cols[row, k]] for k in range(4)], axis=1)
        flat = jnp.concatenate([mask[r, k] for k in range(4)], axis=1)
        total = lax.dot_general(
            picked, flat, (((1,), (1,)), ((), ())), preferred_element_type=F32
        )
        own = joined[row].astype(F32)
        below = degree[0, 0:1, r * LANES : (r + 1) * LANES] + 1.0
        out[:, r * LANES : (r + 1) * LANES] = ((total + own) / below).astype(BF)


def aggregate(shift, me, cols, joined, mask, degree):
    rows = joined.shape[1]
    group = lambda i, me_ref, cols_ref: lax.rem(me_ref[0] + shift, 4) * 4 + i
    return pl.pallas_call(
        functools.partial(aggregate_kernel, shift),
        out_shape=jax.ShapeDtypeStruct((rows, 2048), BF),
        grid_spec=pltpu.PrefetchScalarGridSpec(
            num_scalar_prefetch=2,
            grid=(4,),
            in_specs=[
                pl.BlockSpec(joined.shape, lambda i, *_: (0, 0, 0)),
                pl.BlockSpec((GROUP, 4, LANES, LANES), lambda i, *p: (group(i, *p), 0, 0, 0)),
                pl.BlockSpec((1, 8, GROUP * LANES), lambda i, *p: (group(i, *p), 0, 0)),
            ],
            out_specs=pl.BlockSpec((rows, GROUP * LANES), lambda i, *_: (0, i)),
        ),
        compiler_params=params(),
        cost_estimate=cost(1e8, 4 << 20),
        name="aggregate",
    )(me, cols, joined, mask, degree)


def dense_kernel(me_ref, *refs):
    feats, aggs, ups = refs[0:4], refs[4:8], refs[8:12]
    self_w, neighbor_w, self_t, neighbor_t, bias, degree = refs[12:18]
    hiddens, means, sums, grads = refs[18:22], refs[22:26], refs[26:30], refs[30:34]
    both, up, slope_s, hid_s, mean_s, sum_s, grad_s = refs[34:]
    me = me_ref[0]
    step = pl.program_id(0)
    width = feats[0].shape[1]

    def block(s, size):
        return pl.ds(pl.multiple_of(lax.rem(me + 4 - s, 4) * size, size), size)

    for s in range(4):
        both[block(s, 32), :] = feats[s][...]
        at = pl.ds(pl.multiple_of(128 + lax.rem(me + 4 - s, 4) * 32, 32), 32)
        both[at, :] = aggs[s][...]
        up[block(s, 64), :] = ups[s][...]
    both[256:272, :] = jnp.ones((16, width), BF)
    preact = (
        jnp.dot(self_t[...], both[0:128, :], preferred_element_type=F32)
        + jnp.dot(neighbor_t[...], both[128:256, :], preferred_element_type=F32)
        + bias[...]
    )
    sig = jax.nn.sigmoid(preact)
    hid_s[...] = (preact * sig).astype(BF)
    slope = (up[...].astype(F32) * sig * (1.0 + preact * (1.0 - sig))).astype(BF)
    slope_s[...] = slope
    below = degree[me * 4 + step, 0:1, :] + 1.0
    mean = jnp.dot(neighbor_w[...], slope, preferred_element_type=F32) / below
    mean_s[...] = mean.astype(BF)
    sum_s[...] = (jnp.dot(self_w[...], slope, preferred_element_type=F32) + mean).astype(BF)
    for s in range(4):
        hiddens[s][...] = hid_s[block(s, 64), :]
        means[s][...] = mean_s[block(s, 32), :]
        sums[s][...] = sum_s[block(s, 32), :]
    part = lax.dot_general(
        both[...], slope, (((1,), (1,)), ((), ())), preferred_element_type=F32
    )

    @pl.when(step == 0)
    def _():
        grad_s[...] = part

    @pl.when(step > 0)
    def _():
        grad_s[...] += part

    @pl.when(step == pl.num_programs(0) - 1)
    def _():
        for s in range(4):
            grads[s][0:32, :] = grad_s[block(s, 32), :]
            at = pl.ds(pl.multiple_of(128 + lax.rem(me + 4 - s, 4) * 32, 32), 32)
            grads[s][32:64, :] = grad_s[at, :]
            grads[s][64:72, :] = grad_s[256:264, :]


def dense(me, feats, aggs, ups, weights, bias, degree):
    width = 512
    steps = feats[0].shape[1] // width
    narrow = lambda rows: pl.BlockSpec((rows, width), lambda i: (0, i))
    whole = lambda a: pl.BlockSpec(a.shape, lambda i: (0,) * a.ndim)
    nodes = feats[0].shape[1]
    out = lambda rows: [jax.ShapeDtypeStruct((rows, nodes), BF)] * 4
    got = pl.pallas_call(
        dense_kernel,
        grid=(steps,),
        out_shape=out(64) + out(32) + out(32) + [jax.ShapeDtypeStruct((72, 256), F32)] * 4,
        in_specs=[SMEM]
        + [narrow(32)] * 8
        + [narrow(64)] * 4
        + [whole(w) for w in weights]
        + [whole(bias), whole(degree)],
        out_specs=[narrow(64)] * 4
        + [narrow(32)] * 8
        + [pl.BlockSpec((72, 256), lambda i: (0, 0))] * 4,
        scratch_shapes=[
            pltpu.VMEM((272, width), BF),
            pltpu.VMEM((256, width), BF),
            pltpu.VMEM((256, width), BF),
            pltpu.VMEM((256, width), BF),
            pltpu.VMEM((128, width), BF),
            pltpu.VMEM((128, width), BF),
            pltpu.VMEM((272, 256), F32),
        ],
        compiler_params=params(),
        cost_estimate=cost(1e9, 6 << 20),
        name="dense",
    )(me, *feats, *aggs, *ups, *weights, bias, degree)
    return got[0:4], got[4:8], got[8:12], got[12:16]


def spread_kernel(me_ref, cols, *refs):
    means, mask, local, wire, mean_s, total = refs[0:4], refs[4], refs[5], refs[6], refs[7], refs[8]
    step = pl.program_id(0)
    me = me_ref[0]

    @pl.when(step == 0)
    def _():
        total[...] = jnp.zeros(total.shape, F32)
        for s in range(4):
            first = lax.rem(me + s, 4) * 16
            for t in range(16):
                mean_s[first + t] = means[s][:, t * LANES : (t + 1) * LANES]

    for r in range(GROUP):
        row = step * GROUP + r
        flat = jnp.concatenate([mask[r, k] for k in range(4)], axis=1)
        part = jnp.dot(mean_s[row], flat, preferred_element_type=F32)
        for k in range(4):
            at = cols[row, k]
            total[at] = total[at] + part[:, k * LANES : (k + 1) * LANES]

    @pl.when(step == pl.num_programs(0) - 1)
    def _():
        local[...] = total[0:64]

        @pl.loop(0, 32)
        def _(q):
            wire[2 * q, 0:32, :] = total[64 + 3 * q].astype(BF)
            wire[2 * q + 1, 0:32, :] = total[64 + 3 * q + 2].astype(BF)
            even, odd = split_rest(total[64 + 3 * q + 1])
            wire[2 * q, 32:48, :] = even.astype(BF)
            wire[2 * q + 1, 32:48, :] = odd.astype(BF)
            wire[2 * q, 48:56, :] = jnp.zeros((8, LANES), BF)
            wire[2 * q + 1, 48:56, :] = jnp.zeros((8, LANES), BF)


def spread(me, cols, means, mask):
    whole = lambda shape: pl.BlockSpec(shape, lambda i, *_: (0,) * len(shape))
    rows = means[0].shape[0]
    return pl.pallas_call(
        spread_kernel,
        out_shape=[
            jax.ShapeDtypeStruct((64, rows, LANES), F32),
            jax.ShapeDtypeStruct((64, 56, LANES), BF),
        ],
        grid_spec=pltpu.PrefetchScalarGridSpec(
            num_scalar_prefetch=2,
            grid=(mask.shape[0] // GROUP,),
            in_specs=[whole(means[0].shape)] * 4
            + [pl.BlockSpec((GROUP, 4, LANES, LANES), lambda i, *_: (i, 0, 0, 0))],
            out_specs=[whole((64, rows, LANES)), whole((64, 56, LANES))],
            scratch_shapes=[
                pltpu.VMEM((64, rows, LANES), BF),
                pltpu.VMEM((160, rows, LANES), F32),
            ],
        ),
        compiler_params=params(),
        cost_estimate=cost(5e8, 12 << 20),
        name="spread",
    )(me, cols, *means, mask)


def scatter_kernel(me_ref, idx, wire, local, *refs):
    sums, out, ret, acc = refs[0:4], refs[4], refs[5], refs[6]
    me = me_ref[0]
    fold = local.shape[0] * LANES // CHUNK

    @pl.loop(0, 32)
    def _(q):
        even, odd = wire[2 * q], wire[2 * q + 1]
        ret[2 * q] = even[0:32].astype(F32)
        ret[2 * q + 1] = odd[0:32].astype(F32)
        ret[64 + q] = join_rest(even[32:48].astype(F32), odd[32:48].astype(F32))

    acc[...] = jnp.zeros(acc.shape, F32)

    @pl.loop(0, 12)
    def _(g):
        row = jnp.concatenate([idx[pl.ds(g * 8 + t, 1), :] for t in range(8)], axis=1)
        hi, lo = row >> 9, row & (CHUNK - 1)
        value = jnp.concatenate([ret[g * 8 + t] for t in range(8)], axis=1)
        folded = jnp.concatenate(
            [jnp.where(hi == c, value, 0.0).astype(BF) for c in range(fold)], axis=0
        )
        acc[...] += lax.dot_general(
            folded, one_hot_rows(lo), (((1,), (1,)), ((), ())), preferred_element_type=F32
        )

    for c in range(fold):
        tiles = [local[c * 4 + t] for t in range(4)]
        out[:, c * CHUNK : (c + 1) * CHUNK] = acc[c * 32 : (c + 1) * 32, :] + jnp.concatenate(
            tiles, axis=1
        )
    for s in range(4):
        at = pl.ds(pl.multiple_of(lax.rem(me + s, 4) * 2048, 2048), 2048)
        out[:, at] = out[:, at] + sums[s][...].astype(F32)


def scatter(me, idx, wire, local, sums):
    rows = sums[0].shape[0]
    return pl.pallas_call(
        scatter_kernel,
        out_shape=jax.ShapeDtypeStruct((rows, 8192), F32),
        in_specs=[SMEM] + [VMEM] * 7,
        out_specs=VMEM,
        scratch_shapes=[
            pltpu.VMEM((96, rows, LANES), F32),
            pltpu.VMEM((rows * 16, CHUNK), F32),
        ],
        compiler_params=params(),
        cost_estimate=cost(6.4e9, 5 << 20),
        name="scatter_rows",
    )(me, idx, wire, local, *sums)


def place_kernel(me_ref, a, b, c, d, out):
    for s, piece in enumerate((a, b, c, d)):
        at = pl.ds(pl.multiple_of(lax.rem(me_ref[0] + s, 4) * 2048, 2048), 2048)
        out[:, at] = piece[...]


def place(me, pieces):
    rows = pieces[0].shape[0]
    return pl.pallas_call(
        place_kernel,
        out_shape=jax.ShapeDtypeStruct((rows, 8192), BF),
        in_specs=[SMEM] + [VMEM] * 4,
        out_specs=VMEM,
        compiler_params=params(),
        cost_estimate=cost(1e6, 2 << 20),
        name="place",
    )(me, *pieces)


def exchange(pieces, sign):
    got = [pieces[0]]
    for s in range(1, 4):
        got.append(lax.ppermute(pieces[s], "feat", [(q, (q + sign * s) % 4) for q in range(4)]))
    return got


def per_device(
    quantized,
    node_scale,
    send_rows,
    send_count,
    tile_cols,
    edge_tiles,
    self_weight,
    neighbor_weight,
    hidden_bias,
    upstream,
):
    feat = lax.axis_index("feat")
    dom = lax.axis_index("dom")
    me = feat.astype(jnp.int32).reshape(1)
    cols = tile_cols[0]

    slot = lax.broadcasted_iota(jnp.int32, (64, 192), 1)
    rows = jnp.where(slot < send_count[0][:, None], send_rows[0], -1)
    turned = jnp.concatenate([rows[:, 64:], rows[:, :64]], axis=1)
    rows = jnp.where(dom % 2 == 1, turned, rows)
    idx = jnp.concatenate([rows[:, :128], rows[:, 128:].reshape(32, 128)], axis=0)

    feat_tiles, wire, *feat_blocks = gather(me, quantized, node_scale.reshape(1, -1), idx)
    halo = lax.all_to_all(wire, "dom", split_axis=0, concat_axis=0, tiled=True)

    feats = exchange(feat_blocks, 1)
    up_blocks = [
        lax.dynamic_slice_in_dim(upstream, lax.rem(feat + s, 4) * 2048, 2048, axis=1)
        for s in range(4)
    ]
    ups = exchange(up_blocks, 1)
    small = jnp.concatenate(
        [
            self_weight.astype(F32),
            neighbor_weight.astype(F32),
            jnp.broadcast_to(jnp.pad(hidden_bias, (0, 192))[None, :], (8, 256)),
        ],
        axis=0,
    )
    small = lax.all_gather(small, "feat", axis=0)
    self_w = small[:, 0:32].reshape(128, 256).astype(BF)
    neighbor_w = small[:, 32:64].reshape(128, 256).astype(BF)
    bias = small[:, 64, 0:64].reshape(256, 1)
    weights = [self_w, neighbor_w, self_w.T, neighbor_w.T]

    mask, degree = masks(edge_tiles)
    joined = join(feat_tiles, halo)
    aggs = [None] * 4
    for s in (2, 1, 3, 0):
        aggs[s] = aggregate(s, me, cols, joined, mask, degree)
    aggs = exchange(aggs, 1)
    hiddens, means, sums, grads = dense(me, feats, aggs, ups, weights, bias, degree)
    means = exchange(means, -1)
    grads = exchange(grads, -1)
    means, hiddens, sums = lax.optimization_barrier((means, hiddens, sums))
    local, back = spread(me, cols, means, mask)

    grad = grads[0] + grads[1] + grads[2] + grads[3]
    flat = jnp.concatenate(
        [
            grad[0:64].reshape(2, 64, 128).transpose(1, 0, 2),
            jnp.pad(grad[64].reshape(64, 1, 4), ((0, 0), (0, 0), (0, 124))),
        ],
        axis=1,
    )
    high = flat.astype(BF)
    lower = (flat - high.astype(F32)).astype(BF)
    packed = jnp.concatenate([high, lower, jnp.zeros((64, 2, 128), BF)], axis=1)
    back = back.at[:, 48:56].set(packed)
    returned = lax.all_to_all(back, "dom", split_axis=0, concat_axis=0, tiled=True)

    hidden = place(me, exchange(hiddens, -1))
    sums = exchange(sums, -1)

    arrived = jnp.sum(returned[:, 48:56].astype(F32), axis=0)
    final = jnp.pad(arrived[0:3] + arrived[3:6], ((0, 5), (0, 0)))
    everyone = lax.all_to_all(
        jnp.broadcast_to(final[None], (64, 8, 128)), "dom", split_axis=0, concat_axis=0, tiled=True
    )
    grad_self = everyone[:, 0].reshape(32, 256)
    grad_neighbor = everyone[:, 1].reshape(32, 256)
    grad_bias = lax.dynamic_slice_in_dim(everyone[:, 2, 0:4].reshape(256), feat * 64, 64)
    grad_features = scatter(me, idx, returned, local, sums)
    return hidden, grad_features, grad_self, grad_neighbor, grad_bias


def solution(mesh):
    return jax.shard_map(
        per_device,
        mesh=mesh,
        in_specs=(
            P("feat", "dom"),
            P("dom"),
            P("dom", None, None),
            P("dom", None),
            P("dom", None, None),
            P("dom", None, None, None),
            P("feat", None),
            P("feat", None),
            P("feat"),
            P("feat", "dom"),
        ),
        out_specs=(P("feat", "dom"), P("feat", "dom"), P("feat", None), P("feat", None), P("feat")),
        check_vma=False,
    )
```

```python
import functools

import jax
import jax.numpy as jnp
from jax import lax
from jax.experimental import pallas as pl
from jax.experimental.pallas import tpu as pltpu
from jax.sharding import PartitionSpec as P

BF = jnp.bfloat16
F32 = jnp.float32
VMEM = pl.BlockSpec(memory_space=pltpu.VMEM)
ANY = pl.BlockSpec(memory_space=pl.ANY)
SMEM = pl.BlockSpec(memory_space=pltpu.SMEM)
LANES = 128
GROUP = 4


def params(mib=20):
    return pltpu.CompilerParams(vmem_limit_bytes=mib << 20)


def cost(flops, nbytes):
    return pl.CostEstimate(flops=int(flops), bytes_accessed=int(nbytes), transcendentals=0)


def low_half(shape):
    return lax.broadcasted_iota(jnp.int32, shape, len(shape) - 1) < LANES // 2


def split_rest(tile):
    half = tile.shape[0] // 2
    a, b = tile[:half], tile[half:]
    low = low_half(a.shape)
    even = jnp.where(low, a, pltpu.roll(b, LANES // 2, 1))
    odd = jnp.where(low, pltpu.roll(a, LANES // 2, 1), b)
    return even, odd


def join_rest(even, odd):
    low = low_half(even.shape)
    a = jnp.where(low, even, pltpu.roll(odd, LANES // 2, 1))
    b = jnp.where(low, pltpu.roll(even, LANES // 2, 1), odd)
    return jnp.concatenate([a, b], axis=0)


def one_hot_rows(lo, count):
    rows = lax.broadcasted_iota(jnp.int32, (count, lo.shape[1]), 0)
    return jnp.where(rows == lo, 1.0, 0.0).astype(BF)


class Copies:
    def __init__(self, src, dst, sems, first, parts):
        size = dst.shape[0] // parts
        self.parts = [
            pltpu.make_async_copy(
                src.at[pl.ds(n * size, size)], dst.at[pl.ds(n * size, size)], sems.at[first + n]
            )
            for n in range(parts)
        ]
        for part in self.parts:
            part.start()

    def wait(self):
        for part in self.parts:
            part.wait()


def turn(me, s):
    return lax.rem(me + 4 - s, 4)


def struct(shape, dtype):
    return jax.ShapeDtypeStruct(shape, dtype)


FOLD_IN = 256
FOLD_OUT = 512


def gather_kernel(
    where, quantized, scale, rows, counts, upstream, self_w, neighbor_w, bias,
    tiles_out, wire_out, idx_out, b0, b1, b2, b3,
    q_s, s_s, r_s, c_s, sw_s, nw_s, bias_s, rest_s, folded, feat_tiles, wire, idx, block_s, sems,
):
    pairs = [(scale, s_s), (rows, r_s), (counts, c_s)]
    pairs += [(self_w, sw_s), (neighbor_w, nw_s), (bias, bias_s)]
    for n in range(4):
        at = pl.ds(n * 2048, 2048)
        pairs.append((quantized.at[:, at], q_s.at[:, at]))
    copies = [pltpu.make_async_copy(src, dst, sems.at[n]) for n, (src, dst) in enumerate(pairs)]
    for copy in copies:
        copy.start()
    for copy in copies:
        copy.wait()
    me, odd = where[0], where[1]
    ups = []
    for s in range(4):
        at = pl.ds(pl.multiple_of(lax.rem(me + s, 4) * 2048, 2048), 2048)
        dst = block_s.at[s, pl.ds(32, 64)]
        ups.append(pltpu.make_async_copy(upstream.at[:, at], dst, sems.at[17 + s]))
        ups[s].start()
    feature_count, node_count = q_s.shape
    fold = node_count // FOLD_IN
    for c in range(fold):
        at = pl.ds(c * FOLD_IN, FOLD_IN)
        part = (q_s[:, at].astype(F32) * s_s[:, at]).astype(BF)
        folded[c * feature_count : (c + 1) * feature_count, :] = part
        for t in range(FOLD_IN // LANES):
            feat_tiles[c * (FOLD_IN // LANES) + t] = part[:, t * LANES : (t + 1) * LANES]

    peers = r_s.shape[1]
    spread_counts = jnp.broadcast_to(c_s[...], (peers, peers))
    diagonal = lax.broadcasted_iota(jnp.int32, (peers, peers), 0) == lax.broadcasted_iota(
        jnp.int32, (peers, peers), 1
    )
    limit = jnp.sum(jnp.where(diagonal, spread_counts, 0), axis=1, keepdims=True)
    lane = lax.broadcasted_iota(jnp.int32, (peers, LANES), 1)
    first = jnp.where(lane < limit, r_s[0, :, 0:LANES], -1)
    last = jnp.concatenate(
        [r_s[0, :, LANES : LANES + 64], jnp.full((peers, 64), -1, jnp.int32)], axis=1
    )
    last = jnp.where(lane + LANES < limit, last, -1)
    low = lane < 64
    moved = jnp.where(low, pltpu.roll(first, 64, 1), pltpu.roll(last, 64, 1))
    is_odd = jnp.full((peers, LANES), odd, jnp.int32) == 1
    idx[0:peers, :] = jnp.where(is_odd, moved, first)
    rest_s[...] = jnp.where(is_odd, first, last)
    even_rows = rest_s[pl.ds(0, peers // 2, stride=2), :]
    odd_rows = rest_s[pl.ds(1, peers // 2, stride=2), :]
    idx[peers : peers + peers // 2, :] = jnp.where(
        low[0 : peers // 2], even_rows, pltpu.roll(odd_rows, 64, 1)
    )

    per_block = node_count // 4 // LANES
    for s in range(4):
        begin = lax.rem(me + s, 4) * per_block
        for t in range(per_block):
            block_s[s, 0:32, t * LANES : (t + 1) * LANES] = feat_tiles[begin + t]
    whole_bias = jnp.broadcast_to(bias_s[...], (32, 64))
    for s in range(4):
        block_s[s, 96:128, 512:] = jnp.zeros((32, 1536), BF)
        block_s[s, 96:128, 0:256] = sw_s[...]
        block_s[s, 96:128, 256:512] = nw_s[...]
        left = whole_bias
        for n in range(3):
            part = left.astype(BF)
            block_s[s, 96:128, 512 + n * LANES : 576 + n * LANES] = part
            left = left - part.astype(F32)
    pairs = [(feat_tiles, tiles_out), (idx, idx_out)]
    for s, block in enumerate((b0, b1, b2, b3)):
        pairs.append((block_s.at[s], block))
    for copy in ups:
        copy.wait()
    sends = [
        pltpu.make_async_copy(src, dst, sems.at[21 + n]) for n, (src, dst) in enumerate(pairs)
    ]
    for send in sends:
        send.start()

    def pick(base):
        row = jnp.concatenate([idx[pl.ds(base + t, 1), :] for t in range(8)], axis=1)
        hi, lo = row >> 8, row & (FOLD_IN - 1)
        out = jnp.dot(folded[...], one_hot_rows(lo, FOLD_IN), preferred_element_type=F32)
        total = jnp.zeros((feature_count, row.shape[1]), F32)
        for c in range(fold):
            total = total + jnp.where(hi == c, out[c * feature_count : (c + 1) * feature_count], 0.0)
        return [total[:, t * LANES : (t + 1) * LANES] for t in range(8)]

    @pl.loop(0, 8, unroll=2)
    def _(g):
        tiles = pick(g * 8)
        for t in range(8):
            wire[g * 8 + t, 0:feature_count, :] = tiles[t].astype(BF)

    @pl.loop(0, 4, unroll=2)
    def _(g):
        tiles = pick(64 + g * 8)
        for t in range(8):
            even, odd_part = split_rest(tiles[t])
            wire[(g * 8 + t) * 2, feature_count:48, :] = even.astype(BF)
            wire[(g * 8 + t) * 2 + 1, feature_count:48, :] = odd_part.astype(BF)
        at = pl.ds(g * 16, 16)
        pltpu.make_async_copy(wire.at[at], wire_out.at[at], sems.at[13 + g]).start()

    for send in sends:
        send.wait()
    for g in range(4):
        at = pl.ds(g * 16, 16)
        pltpu.make_async_copy(wire.at[at], wire_out.at[at], sems.at[13 + g]).wait()


def gather(where, quantized, scale, rows, counts, *early):
    features, nodes = quantized.shape
    return pl.pallas_call(
        gather_kernel,
        out_shape=[
            struct((nodes // LANES, features, LANES), BF),
            struct((64, 48, LANES), BF),
            struct((96, LANES), jnp.int32),
        ]
        + [struct((128, nodes // 4), BF)] * 4,
        in_specs=[SMEM] + [ANY] * 8,
        out_specs=[ANY] * 7,
        scratch_shapes=[
            pltpu.VMEM(quantized.shape, BF),
            pltpu.VMEM(scale.shape, F32),
            pltpu.VMEM(rows.shape, jnp.int32),
            pltpu.VMEM(counts.shape, jnp.int32),
            pltpu.VMEM((32, 256), BF),
            pltpu.VMEM((32, 256), BF),
            pltpu.VMEM((1, 64), F32),
            pltpu.VMEM((64, LANES), jnp.int32),
            pltpu.VMEM((features * nodes // FOLD_IN, FOLD_IN), BF),
            pltpu.VMEM((nodes // LANES, features, LANES), BF),
            pltpu.VMEM((64, 48, LANES), BF),
            pltpu.VMEM((96, LANES), jnp.int32),
            pltpu.VMEM((4, 128, nodes // 4), BF),
            pltpu.SemaphoreType.DMA((27,)),
        ],
        compiler_params=params(60),
        cost_estimate=cost(6.4e9, 4 << 20),
        name="gather_rows",
    )(where, quantized, scale, rows, counts, *early)


def mask_kernel(edges, mask, degree, edges_s, mask_s, in_sems, out_sems):
    steps = edges.shape[0] // GROUP
    ones = jnp.ones((8, LANES), BF)
    loads = []
    stores = []
    for i in range(steps):
        at = pl.ds(i * GROUP, GROUP)
        loads.append(pltpu.make_async_copy(edges.at[at], edges_s.at[at], in_sems.at[i]))
        stores.append(pltpu.make_async_copy(mask_s.at[at], mask.at[at], out_sems.at[i]))
        loads[i].start()
    for i in range(steps):
        loads[i].wait()
        for r in range(i * GROUP, (i + 1) * GROUP):
            whole = edges_s[r]
            mask_s[r] = whole.astype(F32).astype(BF)
            total = (whole[0] + whole[1] + whole[2] + whole[3]).astype(F32).astype(BF)
            degree[r] = lax.dot_general(
                ones, total, (((1,), (1,)), ((), ())), preferred_element_type=F32
            )[0:1]
        stores[i].start()
    for store in stores:
        store.wait()


def masks(edges):
    tiles = edges.shape[0]
    length = 6 * tiles
    return pl.pallas_call(
        mask_kernel,
        out_shape=[struct((length,) + edges.shape[1:], BF), struct((tiles, 1, LANES), F32)],
        in_specs=[ANY],
        out_specs=[ANY, VMEM],
        scratch_shapes=[
            pltpu.VMEM(edges.shape, jnp.int32),
            pltpu.VMEM(edges.shape, BF),
            pltpu.SemaphoreType.DMA((tiles // GROUP,)),
            pltpu.SemaphoreType.DMA((tiles // GROUP,)),
        ],
        compiler_params=params(58),
        cost_estimate=cost(1e9, 24 << 20),
        name="mask_degree",
    )(edges)


QUARTER = 16


PARTS = 4


def fetch(me, shift, mask, chunk, sems, first=0):
    begin = lax.rem(me[0] + shift, 4) * QUARTER
    return Copies(mask.at[pl.ds(begin, QUARTER)], chunk, sems, first, PARTS)


CHUNK = struct((QUARTER, 4, LANES, LANES), BF)


def aggregate_tiles(begin, cols, joined, chunk, degree, out):
    totals = []
    for t in range(QUARTER):
        row = begin + t
        picked = jnp.concatenate([joined[cols[row, k]] for k in range(4)], axis=1)
        flat = jnp.concatenate([chunk[t, k] for k in range(4)], axis=1)
        totals.append(
            lax.dot_general(picked, flat, (((1,), (1,)), ((), ())), preferred_element_type=F32)
        )
    for t in range(QUARTER):
        row = begin + t
        out[:, t * LANES : (t + 1) * LANES] = (
            (totals[t] + joined[row].astype(F32)) / (degree[row] + 1.0)
        ).astype(BF)


ORDER = (2, 1, 3)


def aggregate_kernel(me, cols, feat_tiles, wire, degree, mask, *refs):
    outs, (joined, own_chunk, wire_s, chunks, sems) = refs[0:3], refs[3:]
    arriving = Copies(wire, wire_s, sems, 0, 2)
    local = feat_tiles.shape[0]
    own = Copies(feat_tiles, joined.at[pl.ds(0, local)], sems, 2, 1)
    tiles = [
        fetch(me, shift, mask, chunks.at[n], sems, 8 + PARTS * n) for n, shift in enumerate(ORDER)
    ]
    arriving.wait()

    @pl.loop(0, 32, unroll=8)
    def _(q):
        even, odd = wire_s[2 * q], wire_s[2 * q + 1]
        joined[local + 3 * q] = even[0:32]
        joined[local + 3 * q + 2] = odd[0:32]
        joined[local + 3 * q + 1] = join_rest(even[32:48].astype(F32), odd[32:48].astype(F32)).astype(BF)

    own.wait()
    for n, shift in enumerate(ORDER):
        tiles[n].wait()
        begin = lax.rem(me[0] + shift, 4) * QUARTER
        if n == 1:
            later = fetch(me, 0, mask, own_chunk, sems, 8 + PARTS * 3)
        aggregate_tiles(begin, cols, joined, chunks.at[n], degree, outs[shift - 1])
    later.wait()


def aggregate(me, cols, feat_tiles, wire, degree, mask):
    local, rows, _ = feat_tiles.shape
    got = pl.pallas_call(
        aggregate_kernel,
        out_shape=[struct((rows, 2048), BF)] * 3 + [struct((local + 96, rows, LANES), BF), CHUNK],
        in_specs=[SMEM, SMEM, ANY, ANY, VMEM, ANY],
        out_specs=[VMEM] * 5,
        scratch_shapes=[
            pltpu.VMEM(wire.shape, BF),
            pltpu.VMEM((3,) + CHUNK.shape, BF),
            pltpu.SemaphoreType.DMA((8 + PARTS * 4,)),
        ],
        compiler_params=params(),
        cost_estimate=cost(3e9, 12 << 20),
        name="aggregate",
    )(me, cols, feat_tiles, wire, degree, mask)
    return got[0:3], got[3], got[4]


def aggregate_own_kernel(me, cols, joined, chunk, degree, out):
    aggregate_tiles(me[0] * QUARTER, cols, joined, chunk, degree, out)


def aggregate_own(me, cols, joined, chunk, degree):
    return pl.pallas_call(
        aggregate_own_kernel,
        out_shape=struct((joined.shape[1], 2048), BF),
        in_specs=[SMEM, SMEM, VMEM, VMEM, VMEM],
        out_specs=VMEM,
        compiler_params=params(),
        cost_estimate=cost(1e9, 4 << 20),
        name="aggregate_own",
    )(me, cols, joined, chunk, degree)


def dense_kernel(me_ref, *refs):
    pieces, aggs, degree = refs[0:4], refs[4:8], refs[8]
    backs, hiddens, sums = refs[9:13], refs[13:17], refs[17:21]
    stage, agg, slope, hid_s, back_s, sum_s, sems = refs[21:]
    me = me_ref[0]
    both = (((1,), (1,)), ((), ()))
    nodes = slope.shape[1]
    copies = []
    for s in range(4):
        at = pl.ds(pl.multiple_of(turn(me, s) * 32, 32), 32)
        copies.append(pltpu.make_async_copy(aggs[s], agg.at[at, :], sems.at[s]))
        copies.append(pltpu.make_async_copy(pieces[s], stage.at[turn(me, s)], sems.at[4 + s]))
    for copy in copies:
        copy.start()
    for copy in copies:
        copy.wait()

    def joint(first, last, at):
        return jnp.concatenate([stage[b, first:last, at] for b in range(4)], axis=0)

    self_w = joint(96, 128, slice(0, 256))
    neighbor_w = joint(96, 128, slice(256, 512))
    self_t = self_w.astype(F32).T.astype(BF)
    neighbor_t = neighbor_w.astype(F32).T.astype(BF)
    diagonal = lax.broadcasted_iota(jnp.int32, (64, 64), 0) == lax.broadcasted_iota(
        jnp.int32, (64, 64), 1
    )
    columns = []
    for b in range(4):
        row = sum(
            stage[b, 96:112, 512 + n * LANES : 576 + n * LANES].astype(F32) for n in range(3)
        )[0:1]
        square = jnp.where(diagonal, jnp.broadcast_to(row, (64, 64)), 0.0)
        columns.append(jnp.sum(square, axis=1, keepdims=True))
    bias = jnp.concatenate(columns, axis=0)
    sends = []

    def send(pieces, whole, size, first):
        for s in range(4):
            if whole.shape[0] == 4:
                src = whole.at[turn(me, s)]
            else:
                src = whole.at[pl.ds(pl.multiple_of(turn(me, s) * size, size), size), :]
            sends.append(pltpu.make_async_copy(src, pieces[s], sems.at[first + s]))
            sends[-1].start()

    for n in range(4):
        at = slice(n * 512, (n + 1) * 512)
        preact = (
            jnp.dot(self_t, joint(0, 32, at), preferred_element_type=F32)
            + jnp.dot(neighbor_t, agg[:, at], preferred_element_type=F32)
            + bias
        )
        sig = jax.nn.sigmoid(preact)
        hid_s[:, at] = (preact * sig).astype(BF)
        part = (
            joint(32, 96, at).astype(F32) * sig * (1.0 + preact * (1.0 - sig))
        ).astype(BF)
        slope[:, at] = part
        below = jnp.concatenate([degree[me * 16 + n * 4 + t] for t in range(4)], axis=1) + 1.0
        whole = jnp.dot(neighbor_w, part, preferred_element_type=F32) / below
        for b in range(4):
            back_s[b, 0:32, at] = whole[b * 32 : (b + 1) * 32].astype(BF)
        own = jnp.dot(self_w, part, preferred_element_type=F32)
        sum_s[:, at] = (own + whole).astype(BF)
    send(hiddens, hid_s, 64, 12)
    send(sums, sum_s, 32, 16)
    all_nodes = slice(0, nodes)
    feat_grad = lax.dot_general(
        joint(0, 32, all_nodes), slope[...], both, preferred_element_type=F32
    )
    agg_grad = lax.dot_general(agg[...], slope[...], both, preferred_element_type=F32)
    bias_grad = lax.dot_general(
        jnp.ones((8, nodes), BF), slope[...], both, preferred_element_type=F32
    )
    bias_row = bias_grad[0:1]
    high = bias_row.astype(BF).astype(F32)
    for b in range(4):
        for n, grad in enumerate((feat_grad, agg_grad)):
            for h in range(2):
                first = b * 32 + h * 16
                at = slice((2 * n + h) * 256, (2 * n + h + 1) * 256)
                back_s[b, 32:48, at] = grad[first : first + 16].astype(BF)
        back_s[b, 32:48, 1024:1280] = jnp.broadcast_to(high, (16, 256)).astype(BF)
        back_s[b, 32:48, 1280:1536] = jnp.broadcast_to(bias_row - high, (16, 256)).astype(BF)
        back_s[b, 32:48, 1536:] = jnp.zeros((16, nodes - 1536), BF)
    send(backs, back_s, 48, 8)
    for copy in sends:
        copy.wait()


def dense(me, pieces, aggs, degree):
    nodes = aggs[0].shape[1]
    got = pl.pallas_call(
        dense_kernel,
        out_shape=[struct((48, nodes), BF)] * 4
        + [struct((64, nodes), BF)] * 4
        + [struct((32, nodes), BF)] * 4,
        in_specs=[SMEM] + [ANY] * 8 + [VMEM],
        out_specs=[ANY] * 12,
        scratch_shapes=[
            pltpu.VMEM((4, 128, nodes), BF),
            pltpu.VMEM((128, nodes), BF),
            pltpu.VMEM((256, nodes), BF),
            pltpu.VMEM((256, nodes), BF),
            pltpu.VMEM((4, 48, nodes), BF),
            pltpu.VMEM((128, nodes), BF),
            pltpu.SemaphoreType.DMA((20,)),
        ],
        compiler_params=params(56),
        cost_estimate=cost(1e9, 5 << 20),
        name="dense",
    )(me, *pieces, *aggs, degree)
    return got[0:4], got[4:8], got[8:12]


def own_quarter(me, row):
    half = jnp.where(me >= 2, row[:, LANES:], row[:, 0:LANES])
    half = jnp.broadcast_to(half, (8, LANES))
    return jnp.where(lax.rem(me, 2) == 1, pltpu.roll(half, 64, 1), half)[0:1, 0:64]


def pack_grads(me, grad, bias, pack_s):
    row = own_quarter(me, bias)
    diagonal = lax.broadcasted_iota(jnp.int32, (64, 64), 0) == lax.broadcasted_iota(
        jnp.int32, (64, 64), 1
    )
    column = jnp.sum(
        jnp.where(diagonal, jnp.broadcast_to(row, (64, 64)), 0.0), axis=1, keepdims=True
    )
    values = [grad[:, 0:LANES], grad[:, LANES:], jnp.broadcast_to(column, (64, LANES))]
    for n, value in enumerate(values):
        high = value.astype(BF).astype(F32)
        pack_s[:, n, :] = high
        pack_s[:, n + 3, :] = value - high
    for n in (6, 7):
        pack_s[:, n, :] = jnp.zeros((64, LANES), F32)


def spread_tiles(begin, cols, mean, chunk, total):
    for half in range(2):
        parts = []
        for t in range(half * 8, half * 8 + 8):
            flat = jnp.concatenate([chunk[t, k] for k in range(4)], axis=1)
            parts.append(
                jnp.dot(mean[0:32, t * LANES : (t + 1) * LANES], flat, preferred_element_type=F32)
            )
        for t in range(8):
            for k in range(4):
                at = cols[begin + half * 8 + t, k]
                total[at] = total[at] + parts[t][:, k * LANES : (k + 1) * LANES]


def spread_own_kernel(me, cols, mean, chunk, total):
    total[...] = jnp.zeros(total.shape, F32)
    spread_tiles(me[0] * QUARTER, cols, mean, chunk, total)


def spread_own(me, cols, mean, chunk):
    return pl.pallas_call(
        spread_own_kernel,
        out_shape=struct((160, 32, LANES), F32),
        in_specs=[SMEM, SMEM, VMEM, VMEM],
        out_specs=VMEM,
        compiler_params=params(),
        cost_estimate=cost(1e9, 4 << 20),
        name="spread_own",
    )(me, cols, mean, chunk)


def spread_kernel(me, cols, begun, mask, *refs):
    backs, (local, wire_out), refs = refs[0:4], refs[4:6], refs[6:]
    total, chunks, back_s, pack_s, wire, sems = refs
    pieces = []
    for s in range(4):
        pieces.append(pltpu.make_async_copy(backs[s], back_s.at[s], sems.at[s]))
        pieces[-1].start()
    tiles = [fetch(me, s, mask, chunks.at[s - 1], sems, 4 + PARTS * s) for s in (1, 2, 3)]
    total[...] = begun[...]
    for s in (1, 2, 3):
        begin = lax.rem(me[0] + s, 4) * QUARTER
        pieces[s].wait()
        tiles[s - 1].wait()
        spread_tiles(begin, cols, back_s.at[s], chunks.at[s - 1], total)
    own = Copies(total.at[pl.ds(0, 64)], local, sems, 4 + PARTS, 2)
    pieces[0].wait()
    grads = sum(back_s[s, 32:48, 0:1536].astype(F32) for s in range(4))
    grad = jnp.concatenate([grads[:, n * 256 : (n + 1) * 256] for n in range(4)], axis=0)
    pack_grads(me[0], grad, grads[0:1, 1024:1280] + grads[0:1, 1280:1536], pack_s)
    wire[:, 48:56, :] = pack_s[...].astype(BF)

    @pl.loop(0, 32, unroll=8)
    def _(q):
        wire[2 * q, 0:32, :] = total[64 + 3 * q].astype(BF)
        wire[2 * q + 1, 0:32, :] = total[64 + 3 * q + 2].astype(BF)
        even, odd = split_rest(total[64 + 3 * q + 1])
        wire[2 * q, 32:48, :] = even.astype(BF)
        wire[2 * q + 1, 32:48, :] = odd.astype(BF)

    leaving = Copies(wire, wire_out, sems, 0, 4)
    own.wait()
    leaving.wait()


def spread(me, cols, begun, mask, backs):
    _, rows, _ = begun.shape
    return pl.pallas_call(
        spread_kernel,
        out_shape=[struct((64, rows, LANES), F32), struct((64, 56, LANES), BF)],
        in_specs=[SMEM, SMEM, VMEM] + [ANY] * 5,
        out_specs=[ANY] * 2,
        scratch_shapes=[
            pltpu.VMEM(begun.shape, F32),
            pltpu.VMEM((3,) + CHUNK.shape, BF),
            pltpu.VMEM((4,) + backs[0].shape, BF),
            pltpu.VMEM((64, 8, LANES), F32),
            pltpu.VMEM((64, 56, LANES), BF),
            pltpu.SemaphoreType.DMA((4 + PARTS * 4,)),
        ],
        compiler_params=params(),
        cost_estimate=cost(3e9, 12 << 20),
        name="spread",
    )(me, cols, begun, mask, *backs)


def scatter_kernel(me_ref, idx, wire, local, *refs):
    sums, out, wire_s, sum_s, ret, acc, idx_s, own_s, out_s, sems = refs[0:4], *refs[4:]
    me = me_ref[0]
    index = Copies(idx, idx_s, sems, 0, 1)
    first = Copies(wire, wire_s, sems, 1, 2)
    later = [Copies(local, own_s, sems, 5, 2)]
    for s in range(4):
        later.append(Copies(sums[s], sum_s.at[lax.rem(me + s, 4)], sems, 9 + s, 1))
    nodes = out.shape[1]
    fold = nodes // FOLD_OUT
    acc[...] = jnp.zeros(acc.shape, F32)
    index.wait()
    first.wait()

    @pl.loop(0, 32, unroll=8)
    def _(q):
        even, odd = wire_s[2 * q], wire_s[2 * q + 1]
        ret[2 * q] = even[0:32].astype(F32)
        ret[2 * q + 1] = odd[0:32].astype(F32)
        ret[64 + q] = join_rest(even[32:48].astype(F32), odd[32:48].astype(F32))

    @pl.loop(0, 6)
    def _(g):
        row = jnp.concatenate([idx_s[pl.ds(g * 16 + t, 1), :] for t in range(16)], axis=1)
        hi, lo = row >> 9, row & (FOLD_OUT - 1)
        value = jnp.concatenate([ret[g * 16 + t] for t in range(16)], axis=1)
        folded = jnp.concatenate(
            [jnp.where(hi == c, value, 0.0).astype(BF) for c in range(fold)], axis=0
        )
        acc[...] += lax.dot_general(
            folded, one_hot_rows(lo, FOLD_OUT), (((1,), (1,)), ((), ())), preferred_element_type=F32
        )

    for copy in later:
        copy.wait()
    per = FOLD_OUT // LANES
    sends = []
    for quarter in range(4):
        for inner in range(fold // 4):
            c = quarter * (fold // 4) + inner
            inside = inner * FOLD_OUT
            own = jnp.concatenate([own_s[c * per + t] for t in range(per)], axis=1)
            extra = sum_s[quarter, :, inside : inside + FOLD_OUT].astype(F32)
            out_s[:, c * FOLD_OUT : (c + 1) * FOLD_OUT] = acc[c * 32 : (c + 1) * 32, :] + own + extra
        at = pl.ds(quarter * 2048, 2048)
        sends.append(pltpu.make_async_copy(out_s.at[:, at], out.at[:, at], sems.at[13 + quarter]))
        sends[-1].start()
    for send in sends:
        send.wait()


def scatter(me, idx, wire, local, sums):
    rows = sums[0].shape[0]
    return pl.pallas_call(
        scatter_kernel,
        out_shape=struct((rows, 8192), F32),
        in_specs=[SMEM] + [ANY] * 7,
        out_specs=ANY,
        scratch_shapes=[
            pltpu.VMEM(wire.shape, BF),
            pltpu.VMEM((4, rows, 2048), BF),
            pltpu.VMEM((96, rows, LANES), F32),
            pltpu.VMEM((rows * 8192 // FOLD_OUT, FOLD_OUT), F32),
            pltpu.VMEM((96, LANES), jnp.int32),
            pltpu.VMEM((64, rows, LANES), F32),
            pltpu.VMEM((rows, 8192), F32),
            pltpu.SemaphoreType.DMA((17,)),
        ],
        compiler_params=params(60),
        cost_estimate=cost(6.4e9, 5 << 20),
        name="scatter_rows",
    )(me, idx, wire, local, *sums)


def place_kernel(me_ref, a, b, c, d, out):
    for s, piece in enumerate((a, b, c, d)):
        at = pl.ds(pl.multiple_of(lax.rem(me_ref[0] + s, 4) * 2048, 2048), 2048)
        out[:, at] = piece[...]


def place(me, pieces):
    rows = pieces[0].shape[0]
    return pl.pallas_call(
        place_kernel,
        out_shape=struct((rows, 8192), BF),
        in_specs=[SMEM] + [VMEM] * 4,
        out_specs=VMEM,
        compiler_params=params(),
        cost_estimate=cost(1e6, 2 << 20),
        name="place",
    )(me, *pieces)


def final_kernel(returned, final, part_s, sems):
    Copies(returned, part_s, sems, 0, 1).wait()
    total = jnp.sum(part_s[:, 48:56, :].astype(F32), axis=0)
    final[...] = jnp.broadcast_to((total[0:4] + total[3:7])[None], final.shape)


def final_part(returned):
    return pl.pallas_call(
        final_kernel,
        out_shape=struct((64, 4, LANES), F32),
        in_specs=[ANY],
        out_specs=VMEM,
        scratch_shapes=[pltpu.VMEM(returned.shape, BF), pltpu.SemaphoreType.DMA((1,))],
        compiler_params=params(),
        cost_estimate=cost(1e6, 1 << 18),
        name="final_part",
    )(returned)


def unpack_kernel(everyone, grad_self, grad_neighbor, grad_bias, all_s, sem):
    copy = pltpu.make_async_copy(everyone, all_s, sem)
    copy.start()
    copy.wait()
    for h in range(2):
        at = pl.ds(h * LANES, LANES)
        grad_self[:, at] = all_s[0:32, h, :]
        grad_neighbor[:, at] = all_s[32:64, h, :]
    diagonal = lax.broadcasted_iota(jnp.int32, (64, LANES), 0) == lax.broadcasted_iota(
        jnp.int32, (64, LANES), 1
    )
    row = jnp.sum(jnp.where(diagonal, all_s[:, 2, :], 0.0), axis=0, keepdims=True)
    grad_bias[...] = row[:, 0:64]


def unpack(everyone):
    return pl.pallas_call(
        unpack_kernel,
        out_shape=[struct((32, 256), F32)] * 2 + [struct((1, 64), F32)],
        in_specs=[ANY],
        out_specs=[VMEM] * 3,
        scratch_shapes=[pltpu.VMEM(everyone.shape, F32), pltpu.SemaphoreType.DMA(())],
        compiler_params=params(),
        cost_estimate=cost(1e6, 1 << 18),
        name="unpack",
    )(everyone)


def exchange(pieces, sign):
    got = [pieces[0]]
    for s in range(1, 4):
        got.append(lax.ppermute(pieces[s], "feat", [(q, (q + sign * s) % 4) for q in range(4)]))
    return got


def per_device(
    quantized,
    node_scale,
    send_rows,
    send_count,
    tile_cols,
    edge_tiles,
    self_weight,
    neighbor_weight,
    hidden_bias,
    upstream,
):
    feat = lax.axis_index("feat").astype(jnp.int32)
    odd = lax.rem(lax.axis_index("dom").astype(jnp.int32), 2)
    me = feat.reshape(1)
    cols = tile_cols[0]

    feat_tiles, wire, idx, *blocks = gather(
        jnp.stack([feat, odd]),
        quantized,
        node_scale.reshape(1, -1),
        send_rows,
        send_count,
        upstream,
        self_weight,
        neighbor_weight,
        hidden_bias.reshape(1, -1),
    )
    halo = lax.all_to_all(wire, "dom", split_axis=0, concat_axis=0, tiled=True)
    pieces = exchange(blocks, 1)
    mask, degree = masks(edge_tiles)

    others, joined, chunk = aggregate(me, cols, feat_tiles, halo, degree, mask)
    aggs = exchange([aggregate_own(me, cols, joined, chunk, degree), *others], 1)
    backs, hiddens, sums = dense(me, pieces, aggs, degree)
    backs = exchange(backs, -1)
    begun = spread_own(me, cols, backs[0], chunk)
    local, back = spread(me, cols, begun, mask, backs)
    returned = lax.all_to_all(back, "dom", split_axis=0, concat_axis=0, tiled=True)
    local, hiddens, sums = lax.optimization_barrier((local, hiddens, sums))

    hidden = place(me, exchange(hiddens, -1))
    sums = exchange(sums, -1)
    everyone = lax.all_to_all(
        final_part(returned), "dom", split_axis=0, concat_axis=0, tiled=True
    )
    grad_features = scatter(me, idx, returned, local, sums)
    grad_self, grad_neighbor, grad_bias = unpack(everyone)
    return hidden, grad_features, grad_self, grad_neighbor, grad_bias.reshape(-1)


def solution(mesh):
    return jax.shard_map(
        per_device,
        mesh=mesh,
        in_specs=(
            P("feat", "dom"),
            P("dom"),
            P("dom", None, None),
            P("dom", None),
            P("dom", None, None),
            P("dom", None, None, None),
            P("feat", None),
            P("feat", None),
            P("feat"),
            P("feat", "dom"),
        ),
        out_specs=(P("feat", "dom"), P("feat", "dom"), P("feat", None), P("feat", None), P("feat")),
        check_vma=False,
    )
```

```python
import functools

import jax
import jax.numpy as jnp
from jax import lax
from jax.experimental import pallas as pl
from jax.experimental.pallas import tpu as pltpu
from jax.sharding import PartitionSpec as P

BF = jnp.bfloat16
F32 = jnp.float32
VMEM = pl.BlockSpec(memory_space=pltpu.VMEM)
ANY = pl.BlockSpec(memory_space=pl.ANY)
SMEM = pl.BlockSpec(memory_space=pltpu.SMEM)
LANES = 128
GROUP = 4


def params(mib=48):
    return pltpu.CompilerParams(vmem_limit_bytes=mib << 20)


def cost(flops, nbytes):
    return pl.CostEstimate(flops=int(flops), bytes_accessed=int(nbytes), transcendentals=0)


def low_half(shape):
    return lax.broadcasted_iota(jnp.int32, shape, len(shape) - 1) < LANES // 2


def split_rest(tile):
    half = tile.shape[0] // 2
    a, b = tile[:half], tile[half:]
    low = low_half(a.shape)
    even = jnp.where(low, a, pltpu.roll(b, LANES // 2, 1))
    odd = jnp.where(low, pltpu.roll(a, LANES // 2, 1), b)
    return even, odd


def join_rest(even, odd):
    low = low_half(even.shape)
    a = jnp.where(low, even, pltpu.roll(odd, LANES // 2, 1))
    b = jnp.where(low, pltpu.roll(even, LANES // 2, 1), odd)
    return jnp.concatenate([a, b], axis=0)


def one_hot_rows(lo, count):
    rows = lax.broadcasted_iota(jnp.int32, (count, lo.shape[1]), 0)
    return jnp.where(rows == lo, 1.0, 0.0).astype(BF)


class Copies:
    def __init__(self, src, dst, sems, first, parts):
        size = dst.shape[0] // parts
        self.parts = [
            pltpu.make_async_copy(
                src.at[pl.ds(n * size, size)], dst.at[pl.ds(n * size, size)], sems.at[first + n]
            )
            for n in range(parts)
        ]
        for part in self.parts:
            part.start()

    def wait(self):
        for part in self.parts:
            part.wait()


def turn(me, s):
    return lax.rem(me + 4 - s, 4)


def struct(shape, dtype):
    return jax.ShapeDtypeStruct(shape, dtype)


DEGREE_ROWS = 36864
LOCAL_TILES = 1152


FOLD_IN = 256
FOLD_OUT = 512


def gather_kernel(
    quantized, scale, rows, counts, upstream, self_w, neighbor_w, bias,
    tiles_out, wire_out, idx_out, b0, b1, b2, b3,
    q_s, s_s, r_s, c_s, sw_s, nw_s, bias_s, rest_s, folded, feat_tiles, wire, idx, block_s, sems,
):
    pairs = [(scale, s_s), (rows, r_s), (counts, c_s)]
    pairs += [(self_w, sw_s), (neighbor_w, nw_s), (bias, bias_s)]
    for n in range(4):
        at = pl.ds(n * 2048, 2048)
        pairs.append((quantized.at[:, at], q_s.at[:, at]))
    copies = [pltpu.make_async_copy(src, dst, sems.at[n]) for n, (src, dst) in enumerate(pairs)]
    for copy in copies:
        copy.start()
    for copy in copies:
        copy.wait()
    me = lax.axis_index("feat").astype(jnp.int32)
    odd = lax.rem(lax.axis_index("dom").astype(jnp.int32), 2)
    ups = []
    for s in range(4):
        at = pl.ds(pl.multiple_of(lax.rem(me + s, 4) * 2048, 2048), 2048)
        dst = block_s.at[s, pl.ds(32, 64)]
        ups.append(pltpu.make_async_copy(upstream.at[:, at], dst, sems.at[17 + s]))
        ups[s].start()
    feature_count, node_count = q_s.shape
    fold = node_count // FOLD_IN
    for c in range(fold):
        at = pl.ds(c * FOLD_IN, FOLD_IN)
        part = (q_s[:, at].astype(F32) * s_s[:, at]).astype(BF)
        folded[c * feature_count : (c + 1) * feature_count, :] = part
        for t in range(FOLD_IN // LANES):
            feat_tiles[c * (FOLD_IN // LANES) + t] = part[:, t * LANES : (t + 1) * LANES]

    peers = r_s.shape[1]
    spread_counts = jnp.broadcast_to(c_s[...], (peers, peers))
    diagonal = lax.broadcasted_iota(jnp.int32, (peers, peers), 0) == lax.broadcasted_iota(
        jnp.int32, (peers, peers), 1
    )
    limit = jnp.sum(jnp.where(diagonal, spread_counts, 0), axis=1, keepdims=True)
    lane = lax.broadcasted_iota(jnp.int32, (peers, LANES), 1)
    first = jnp.where(lane < limit, r_s[0, :, 0:LANES], -1)
    last = jnp.concatenate(
        [r_s[0, :, LANES : LANES + 64], jnp.full((peers, 64), -1, jnp.int32)], axis=1
    )
    last = jnp.where(lane + LANES < limit, last, -1)
    low = lane < 64
    moved = jnp.where(low, pltpu.roll(first, 64, 1), pltpu.roll(last, 64, 1))
    is_odd = jnp.full((peers, LANES), odd, jnp.int32) == 1
    idx[0:peers, :] = jnp.where(is_odd, moved, first)
    rest_s[...] = jnp.where(is_odd, first, last)
    even_rows = rest_s[pl.ds(0, peers // 2, stride=2), :]
    odd_rows = rest_s[pl.ds(1, peers // 2, stride=2), :]
    idx[peers : peers + peers // 2, :] = jnp.where(
        low[0 : peers // 2], even_rows, pltpu.roll(odd_rows, 64, 1)
    )

    per_block = node_count // 4 // LANES
    for s in range(4):
        begin = lax.rem(me + s, 4) * per_block
        for t in range(per_block):
            block_s[s, 0:32, t * LANES : (t + 1) * LANES] = feat_tiles[begin + t]
    whole_bias = jnp.broadcast_to(bias_s[...], (32, 64))
    for s in range(4):
        block_s[s, 96:128, 512:] = jnp.zeros((32, 1536), BF)
        block_s[s, 96:128, 0:256] = sw_s[...]
        block_s[s, 96:128, 256:512] = nw_s[...]
        left = whole_bias
        for n in range(3):
            part = left.astype(BF)
            block_s[s, 96:128, 512 + n * LANES : 576 + n * LANES] = part
            left = left - part.astype(F32)
    pairs = [(feat_tiles, tiles_out), (idx, idx_out)]
    for s, block in enumerate((b0, b1, b2, b3)):
        pairs.append((block_s.at[s], block))
    for copy in ups:
        copy.wait()
    sends = [
        pltpu.make_async_copy(src, dst, sems.at[21 + n]) for n, (src, dst) in enumerate(pairs)
    ]
    for send in sends:
        send.start()

    def pick(base):
        row = jnp.concatenate([idx[pl.ds(base + t, 1), :] for t in range(16)], axis=1)
        hi, lo = row >> 8, row & (FOLD_IN - 1)
        out = jnp.dot(folded[...], one_hot_rows(lo, FOLD_IN), preferred_element_type=F32)
        total = jnp.zeros((feature_count, row.shape[1]), F32)
        for c in range(fold):
            total = total + jnp.where(hi == c, out[c * feature_count : (c + 1) * feature_count], 0.0)
        return [total[:, t * LANES : (t + 1) * LANES] for t in range(16)]

    @pl.loop(0, 4, unroll=2)
    def _(g):
        tiles = pick(g * 16)
        for t in range(16):
            wire[g * 16 + t, 0:feature_count, :] = tiles[t].astype(BF)

    @pl.loop(0, 2, unroll=2)
    def _(g):
        tiles = pick(64 + g * 16)
        for t in range(16):
            even, odd_part = split_rest(tiles[t])
            wire[(g * 16 + t) * 2, feature_count:48, :] = even.astype(BF)
            wire[(g * 16 + t) * 2 + 1, feature_count:48, :] = odd_part.astype(BF)
        at = pl.ds(g * 32, 32)
        pltpu.make_async_copy(wire.at[at], wire_out.at[at], sems.at[13 + g]).start()

    for send in sends:
        send.wait()
    for g in range(2):
        at = pl.ds(g * 32, 32)
        pltpu.make_async_copy(wire.at[at], wire_out.at[at], sems.at[13 + g]).wait()


def gather(quantized, scale, rows, counts, *early):
    features, nodes = quantized.shape
    return pl.pallas_call(
        gather_kernel,
        out_shape=[
            struct((nodes // LANES, features, LANES), BF),
            struct((64, 48, LANES), BF),
            struct((96, LANES), jnp.int32),
        ]
        + [struct((128, nodes // 4), BF)] * 4,
        in_specs=[ANY] * 8,
        out_specs=[ANY] * 7,
        scratch_shapes=[
            pltpu.VMEM(quantized.shape, BF),
            pltpu.VMEM(scale.shape, F32),
            pltpu.VMEM(rows.shape, jnp.int32),
            pltpu.VMEM(counts.shape, jnp.int32),
            pltpu.VMEM((32, 256), BF),
            pltpu.VMEM((32, 256), BF),
            pltpu.VMEM((1, 64), F32),
            pltpu.VMEM((64, LANES), jnp.int32),
            pltpu.VMEM((features * nodes // FOLD_IN, FOLD_IN), BF),
            pltpu.VMEM((nodes // LANES, features, LANES), BF),
            pltpu.VMEM((64, 48, LANES), BF),
            pltpu.VMEM((96, LANES), jnp.int32),
            pltpu.VMEM((4, 128, nodes // 4), BF),
            pltpu.SemaphoreType.DMA((27,)),
        ],
        compiler_params=params(60),
        cost_estimate=cost(6.4e9, 4 << 20),
        name="gather_rows",
    )(quantized, scale, rows, counts, *early)


def mask_kernel(edges, mask, degree_out, edges_s, mask_s, degree, in_sems, out_sems):
    steps = edges.shape[0] // GROUP
    ones = jnp.ones((8, LANES), BF)
    loads = []
    stores = []
    for i in range(steps):
        at = pl.ds(i * GROUP, GROUP)
        loads.append(pltpu.make_async_copy(edges.at[at], edges_s.at[at], in_sems.at[i]))
        stores.append(pltpu.make_async_copy(mask_s.at[at], mask.at[at], out_sems.at[i]))
        loads[i].start()
    for i in range(steps):
        loads[i].wait()
        for r in range(i * GROUP, (i + 1) * GROUP):
            whole = edges_s[r]
            mask_s[r] = whole.astype(F32).astype(BF)
            total = (whole[0] + whole[1] + whole[2] + whole[3]).astype(F32).astype(BF)
            degree[r] = lax.dot_general(
                ones, total, (((1,), (1,)), ((), ())), preferred_element_type=F32
            )[0:1]
        stores[i].start()
    stores.append(
        pltpu.make_async_copy(degree, degree_out.at[pl.ds(0, degree.shape[0])], in_sems.at[0])
    )
    stores[-1].start()
    for store in stores:
        store.wait()


def masks(edges):
    tiles = edges.shape[0]
    length = 3 * tiles
    return pl.pallas_call(
        mask_kernel,
        out_shape=[struct((length,) + edges.shape[1:], BF), struct((DEGREE_ROWS, 1, LANES), F32)],
        in_specs=[ANY],
        out_specs=[ANY, ANY],
        scratch_shapes=[
            pltpu.VMEM(edges.shape, jnp.int32),
            pltpu.VMEM(edges.shape, BF),
            pltpu.VMEM((tiles, 1, LANES), F32),
            pltpu.SemaphoreType.DMA((tiles // GROUP,)),
            pltpu.SemaphoreType.DMA((tiles // GROUP,)),
        ],
        compiler_params=params(58),
        cost_estimate=cost(1e9, 24 << 20),
        name="mask_degree",
    )(edges)


QUARTER = 16


PARTS = 4


def fetch(me, shift, mask, chunk, sems, first=0):
    begin = lax.rem(me[0] + shift, 4) * QUARTER
    return Copies(mask.at[pl.ds(begin, QUARTER)], chunk, sems, first, PARTS)


CHUNK = struct((QUARTER, 4, LANES, LANES), BF)


def aggregate_tiles(begin, cols, joined, chunk, degree, out):
    totals = []
    for t in range(QUARTER):
        row = begin + t
        picked = jnp.concatenate([joined[cols[row, k]] for k in range(4)], axis=1)
        flat = jnp.concatenate([chunk[t, k] for k in range(4)], axis=1)
        totals.append(
            lax.dot_general(picked, flat, (((1,), (1,)), ((), ())), preferred_element_type=F32)
        )
    for t in range(QUARTER):
        row = begin + t
        out[:, t * LANES : (t + 1) * LANES] = (
            (totals[t] + joined[row].astype(F32)) / (degree[row] + 1.0)
        ).astype(BF)


ORDER = (2, 1, 3)


def aggregate_kernel(me, cols, feat_tiles, wire, degree_in, mask, *refs):
    outs, (joined, own_chunk, degree, wire_s, chunks, sems) = refs[0:3], refs[3:]
    arriving = Copies(wire, wire_s, sems, 0, 2)
    counts = Copies(degree_in.at[pl.ds(0, 64)], degree, sems, 3, 1)
    local = 64
    own = Copies(feat_tiles, joined.at[pl.ds(0, local)], sems, 2, 1)
    tiles = [
        fetch(me, shift, mask, chunks.at[n], sems, 8 + PARTS * n) for n, shift in enumerate(ORDER)
    ]
    arriving.wait()

    @pl.loop(0, 32, unroll=8)
    def _(q):
        even, odd = wire_s[2 * q], wire_s[2 * q + 1]
        joined[local + 3 * q] = even[0:32]
        joined[local + 3 * q + 2] = odd[0:32]
        joined[local + 3 * q + 1] = join_rest(even[32:48].astype(F32), odd[32:48].astype(F32)).astype(BF)

    own.wait()
    counts.wait()
    for n, shift in enumerate(ORDER):
        tiles[n].wait()
        begin = lax.rem(me[0] + shift, 4) * QUARTER
        if n == 1:
            later = fetch(me, 0, mask, own_chunk, sems, 8 + PARTS * 3)
        aggregate_tiles(begin, cols, joined, chunks.at[n], degree, outs[shift - 1])
    later.wait()


def aggregate(me, cols, feat_tiles, wire, degree, mask):
    rows = feat_tiles.shape[1]
    got = pl.pallas_call(
        aggregate_kernel,
        out_shape=[struct((rows, 2048), BF)] * 3 + [struct((160, rows, LANES), BF), CHUNK]
        + [struct((64, 1, LANES), F32)],
        in_specs=[SMEM, SMEM] + [ANY] * 4,
        out_specs=[VMEM] * 6,
        scratch_shapes=[
            pltpu.VMEM(wire.shape, BF),
            pltpu.VMEM((3,) + CHUNK.shape, BF),
            pltpu.SemaphoreType.DMA((8 + PARTS * 4,)),
        ],
        compiler_params=params(),
        cost_estimate=cost(3e9, 12 << 20),
        name="aggregate",
    )(me, cols, feat_tiles, wire, degree, mask)
    return got[0:3], got[3], got[4], got[5]


def aggregate_own_kernel(me, cols, joined, chunk, degree, out):
    aggregate_tiles(me[0] * QUARTER, cols, joined, chunk, degree, out)


def aggregate_own(me, cols, joined, chunk, degree):
    return pl.pallas_call(
        aggregate_own_kernel,
        out_shape=struct((joined.shape[1], 2048), BF),
        in_specs=[SMEM, SMEM, VMEM, VMEM, VMEM],
        out_specs=VMEM,
        compiler_params=params(),
        cost_estimate=cost(1e9, 4 << 20),
        name="aggregate_own",
    )(me, cols, joined, chunk, degree)


def dense_kernel(me_ref, *refs):
    pieces, aggs, degree = refs[0:4], refs[4:8], refs[8]
    backs, hiddens, sums = refs[9:13], refs[13:17], refs[17:21]
    stage, agg, slope, hid_s, back_s, sum_s, sems = refs[21:]
    me = me_ref[0]
    both = (((1,), (1,)), ((), ()))
    nodes = slope.shape[1]
    copies = []
    for s in range(4):
        at = pl.ds(pl.multiple_of(turn(me, s) * 32, 32), 32)
        copies.append(pltpu.make_async_copy(aggs[s], agg.at[at, :], sems.at[s]))
        copies.append(pltpu.make_async_copy(pieces[s], stage.at[turn(me, s)], sems.at[4 + s]))
    for copy in copies:
        copy.start()
    for copy in copies:
        copy.wait()

    def joint(first, last, at):
        return jnp.concatenate([stage[b, first:last, at] for b in range(4)], axis=0)

    self_w = joint(96, 128, slice(0, 256))
    neighbor_w = joint(96, 128, slice(256, 512))
    self_t = self_w.astype(F32).T.astype(BF)
    neighbor_t = neighbor_w.astype(F32).T.astype(BF)
    diagonal = lax.broadcasted_iota(jnp.int32, (64, 64), 0) == lax.broadcasted_iota(
        jnp.int32, (64, 64), 1
    )
    columns = []
    for b in range(4):
        row = sum(
            stage[b, 96:112, 512 + n * LANES : 576 + n * LANES].astype(F32) for n in range(3)
        )[0:1]
        square = jnp.where(diagonal, jnp.broadcast_to(row, (64, 64)), 0.0)
        columns.append(jnp.sum(square, axis=1, keepdims=True))
    bias = jnp.concatenate(columns, axis=0)
    sends = []

    def send(pieces, whole, size, first):
        for s in range(4):
            if whole.shape[0] == 4:
                src = whole.at[turn(me, s)]
            else:
                src = whole.at[pl.ds(pl.multiple_of(turn(me, s) * size, size), size), :]
            sends.append(pltpu.make_async_copy(src, pieces[s], sems.at[first + s]))
            sends[-1].start()

    for n in range(4):
        at = slice(n * 512, (n + 1) * 512)
        preact = (
            jnp.dot(self_t, joint(0, 32, at), preferred_element_type=F32)
            + jnp.dot(neighbor_t, agg[:, at], preferred_element_type=F32)
            + bias
        )
        sig = jax.nn.sigmoid(preact)
        hid_s[:, at] = (preact * sig).astype(BF)
        part = (
            joint(32, 96, at).astype(F32) * sig * (1.0 + preact * (1.0 - sig))
        ).astype(BF)
        slope[:, at] = part
        below = jnp.concatenate([degree[me * 16 + n * 4 + t] for t in range(4)], axis=1) + 1.0
        whole = jnp.dot(neighbor_w, part, preferred_element_type=F32) / below
        for b in range(4):
            back_s[b, 0:32, at] = whole[b * 32 : (b + 1) * 32].astype(BF)
        own = jnp.dot(self_w, part, preferred_element_type=F32)
        sum_s[:, at] = (own + whole).astype(BF)
    send(hiddens, hid_s, 64, 12)
    send(sums, sum_s, 32, 16)
    all_nodes = slice(0, nodes)
    feat_grad = lax.dot_general(
        joint(0, 32, all_nodes), slope[...], both, preferred_element_type=F32
    )
    agg_grad = lax.dot_general(agg[...], slope[...], both, preferred_element_type=F32)
    bias_grad = lax.dot_general(
        jnp.ones((8, nodes), BF), slope[...], both, preferred_element_type=F32
    )
    bias_row = bias_grad[0:1]
    high = bias_row.astype(BF).astype(F32)
    for b in range(4):
        for n, grad in enumerate((feat_grad, agg_grad)):
            for h in range(4):
                first = b * 32 + h * 8
                at = slice((4 * n + h) * 256, (4 * n + h + 1) * 256)
                back_s[b, 32:40, at] = grad[first : first + 8].astype(BF)
        own = slice(b * 64, (b + 1) * 64)
        both_parts = jnp.concatenate([high[:, own], (bias_row - high)[:, own]], axis=1)
        back_s[b, 0:32, nodes:] = jnp.zeros((32, LANES), BF)
        back_s[b, 32:40, nodes:] = jnp.broadcast_to(both_parts, (8, LANES)).astype(BF)
    send(backs, back_s, 40, 8)
    for copy in sends:
        copy.wait()


def dense(me, pieces, aggs, degree):
    nodes = aggs[0].shape[1]
    got = pl.pallas_call(
        dense_kernel,
        out_shape=[struct((40, nodes + LANES), BF)] * 4
        + [struct((64, nodes), BF)] * 4
        + [struct((32, nodes), BF)] * 4,
        in_specs=[SMEM] + [ANY] * 8 + [VMEM],
        out_specs=[ANY] * 12,
        scratch_shapes=[
            pltpu.VMEM((4, 128, nodes), BF),
            pltpu.VMEM((128, nodes), BF),
            pltpu.VMEM((256, nodes), BF),
            pltpu.VMEM((256, nodes), BF),
            pltpu.VMEM((4, 40, nodes + LANES), BF),
            pltpu.VMEM((128, nodes), BF),
            pltpu.SemaphoreType.DMA((20,)),
        ],
        compiler_params=params(56),
        cost_estimate=cost(1e9, 5 << 20),
        name="dense",
    )(me, *pieces, *aggs, degree)
    return got[0:4], got[4:8], got[8:12]


def pack_grads(grad, row, pack_s):
    diagonal = lax.broadcasted_iota(jnp.int32, (64, 64), 0) == lax.broadcasted_iota(
        jnp.int32, (64, 64), 1
    )
    column = jnp.sum(
        jnp.where(diagonal, jnp.broadcast_to(row, (64, 64)), 0.0), axis=1, keepdims=True
    )
    values = [grad[:, 0:LANES], grad[:, LANES:], jnp.broadcast_to(column, (64, LANES))]
    for n, value in enumerate(values):
        high = value.astype(BF).astype(F32)
        pack_s[:, n, :] = high
        pack_s[:, n + 3, :] = value - high
    for n in (6, 7):
        pack_s[:, n, :] = jnp.zeros((64, LANES), F32)


def spread_tiles(begin, cols, mean, chunk, total):
    for half in range(2):
        parts = []
        for t in range(half * 8, half * 8 + 8):
            flat = jnp.concatenate([chunk[t, k] for k in range(4)], axis=1)
            parts.append(
                jnp.dot(mean[0:32, t * LANES : (t + 1) * LANES], flat, preferred_element_type=F32)
            )
        for t in range(8):
            for k in range(4):
                at = cols[begin + half * 8 + t, k]
                total[at] = total[at] + parts[t][:, k * LANES : (k + 1) * LANES]


def spread_own_kernel(me, cols, mean, chunk, total):
    total[...] = jnp.zeros(total.shape, F32)
    spread_tiles(me[0] * QUARTER, cols, mean, chunk, total)


def spread_own(me, cols, mean, chunk):
    return pl.pallas_call(
        spread_own_kernel,
        out_shape=struct((160, 32, LANES), F32),
        in_specs=[SMEM, SMEM, VMEM, VMEM],
        out_specs=VMEM,
        compiler_params=params(),
        cost_estimate=cost(1e9, 4 << 20),
        name="spread_own",
    )(me, cols, mean, chunk)


def spread_kernel(me, cols, begun, mask, *refs):
    backs, (local, wire_out), refs = refs[0:4], refs[4:6], refs[6:]
    total, chunks, back_s, pack_s, wire, sems = refs
    pieces = []
    for s in range(4):
        pieces.append(pltpu.make_async_copy(backs[s], back_s.at[s], sems.at[s]))
        pieces[-1].start()
    tiles = [fetch(me, s, mask, chunks.at[s - 1], sems, 4 + PARTS * s) for s in (1, 2, 3)]
    total[...] = begun[...]
    for s in (1, 2, 3):
        begin = lax.rem(me[0] + s, 4) * QUARTER
        pieces[s].wait()
        tiles[s - 1].wait()
        spread_tiles(begin, cols, back_s.at[s], chunks.at[s - 1], total)
    own = Copies(total.at[pl.ds(0, 64)], local.at[pl.ds(0, 64)], sems, 4 + PARTS, 2)
    pieces[0].wait()
    grads = sum(back_s[s, 32:40, :].astype(F32) for s in range(4))
    grad = jnp.concatenate([grads[:, n * 256 : (n + 1) * 256] for n in range(8)], axis=0)
    pack_grads(grad, grads[0:1, 2048:2112] + grads[0:1, 2112:2176], pack_s)
    wire[:, 48:56, :] = pack_s[...].astype(BF)

    @pl.loop(0, 32, unroll=8)
    def _(q):
        wire[2 * q, 0:32, :] = total[64 + 3 * q].astype(BF)
        wire[2 * q + 1, 0:32, :] = total[64 + 3 * q + 2].astype(BF)
        even, odd = split_rest(total[64 + 3 * q + 1])
        wire[2 * q, 32:48, :] = even.astype(BF)
        wire[2 * q + 1, 32:48, :] = odd.astype(BF)

    leaving = Copies(wire, wire_out, sems, 0, 4)
    own.wait()
    leaving.wait()


def spread(me, cols, begun, mask, backs):
    _, rows, _ = begun.shape
    return pl.pallas_call(
        spread_kernel,
        out_shape=[struct((LOCAL_TILES, rows, LANES), F32), struct((64, 56, LANES), BF)],
        in_specs=[SMEM, SMEM, VMEM] + [ANY] * 5,
        out_specs=[ANY] * 2,
        scratch_shapes=[
            pltpu.VMEM(begun.shape, F32),
            pltpu.VMEM((3,) + CHUNK.shape, BF),
            pltpu.VMEM((4,) + backs[0].shape, BF),
            pltpu.VMEM((64, 8, LANES), F32),
            pltpu.VMEM((64, 56, LANES), BF),
            pltpu.SemaphoreType.DMA((4 + PARTS * 4,)),
        ],
        compiler_params=params(),
        cost_estimate=cost(3e9, 12 << 20),
        name="spread",
    )(me, cols, begun, mask, *backs)


def scatter_kernel(me_ref, idx, wire, local, *refs):
    sums, out, wire_s, sum_s, ret, acc, idx_s, own_s, out_s, sems = refs[0:4], *refs[4:]
    me = me_ref[0]
    index = Copies(idx, idx_s, sems, 0, 1)
    first = Copies(wire, wire_s, sems, 1, 2)
    later = [Copies(local.at[pl.ds(0, 64)], own_s, sems, 5, 2)]
    for s in range(4):
        later.append(Copies(sums[s], sum_s.at[lax.rem(me + s, 4)], sems, 9 + s, 1))
    nodes = out.shape[1]
    fold = nodes // FOLD_OUT
    acc[...] = jnp.zeros(acc.shape, F32)
    index.wait()
    first.wait()

    @pl.loop(0, 32, unroll=8)
    def _(q):
        even, odd = wire_s[2 * q], wire_s[2 * q + 1]
        ret[2 * q] = even[0:32].astype(F32)
        ret[2 * q + 1] = odd[0:32].astype(F32)
        ret[64 + q] = join_rest(even[32:48].astype(F32), odd[32:48].astype(F32))

    @pl.loop(0, 6, unroll=2)
    def _(g):
        row = jnp.concatenate([idx_s[pl.ds(g * 16 + t, 1), :] for t in range(16)], axis=1)
        hi, lo = row >> 9, row & (FOLD_OUT - 1)
        value = jnp.concatenate([ret[g * 16 + t] for t in range(16)], axis=1)
        folded = jnp.concatenate(
            [jnp.where(hi == c, value, 0.0).astype(BF) for c in range(fold)], axis=0
        )
        acc[...] += lax.dot_general(
            folded, one_hot_rows(lo, FOLD_OUT), (((1,), (1,)), ((), ())), preferred_element_type=F32
        )

    for copy in later:
        copy.wait()
    per = FOLD_OUT // LANES
    sends = []
    for quarter in range(4):
        for inner in range(fold // 4):
            c = quarter * (fold // 4) + inner
            inside = inner * FOLD_OUT
            own = jnp.concatenate([own_s[c * per + t] for t in range(per)], axis=1)
            extra = sum_s[quarter, :, inside : inside + FOLD_OUT].astype(F32)
            out_s[:, c * FOLD_OUT : (c + 1) * FOLD_OUT] = acc[c * 32 : (c + 1) * 32, :] + own + extra
        at = pl.ds(quarter * 2048, 2048)
        sends.append(pltpu.make_async_copy(out_s.at[:, at], out.at[:, at], sems.at[13 + quarter]))
        sends[-1].start()
    for send in sends:
        send.wait()


def scatter(me, idx, wire, local, sums):
    rows = sums[0].shape[0]
    return pl.pallas_call(
        scatter_kernel,
        out_shape=struct((rows, 8192), F32),
        in_specs=[SMEM] + [ANY] * 7,
        out_specs=ANY,
        scratch_shapes=[
            pltpu.VMEM(wire.shape, BF),
            pltpu.VMEM((4, rows, 2048), BF),
            pltpu.VMEM((96, rows, LANES), F32),
            pltpu.VMEM((rows * 8192 // FOLD_OUT, FOLD_OUT), F32),
            pltpu.VMEM((96, LANES), jnp.int32),
            pltpu.VMEM((64, rows, LANES), F32),
            pltpu.VMEM((rows, 8192), F32),
            pltpu.SemaphoreType.DMA((17,)),
        ],
        compiler_params=params(),
        cost_estimate=cost(6.4e9, 5 << 20),
        name="scatter_rows",
    )(me, idx, wire, local, *sums)


def place_kernel(me_ref, a, b, c, d, out):
    for s, piece in enumerate((a, b, c, d)):
        at = pl.ds(pl.multiple_of(lax.rem(me_ref[0] + s, 4) * 2048, 2048), 2048)
        out[:, at] = piece[...]


def place(me, pieces):
    rows = pieces[0].shape[0]
    return pl.pallas_call(
        place_kernel,
        out_shape=struct((rows, 8192), BF),
        in_specs=[SMEM] + [VMEM] * 4,
        out_specs=VMEM,
        compiler_params=params(),
        cost_estimate=cost(1e6, 2 << 20),
        name="place",
    )(me, *pieces)


def final_kernel(returned, final):
    total = jnp.sum(returned[:, 48:56, :].astype(F32), axis=0)
    final[...] = jnp.broadcast_to((total[0:4] + total[3:7])[None], final.shape)


def final_part(returned):
    return pl.pallas_call(
        final_kernel,
        out_shape=struct((64, 4, LANES), F32),
        in_specs=[VMEM],
        out_specs=VMEM,
        compiler_params=params(),
        cost_estimate=cost(1e6, 1 << 18),
        name="final_part",
    )(returned)


def unpack_kernel(everyone, grad_self, grad_neighbor, grad_bias, all_s, sem):
    copy = pltpu.make_async_copy(everyone, all_s, sem)
    copy.start()
    copy.wait()
    for h in range(2):
        at = pl.ds(h * LANES, LANES)
        grad_self[:, at] = all_s[0:32, h, :]
        grad_neighbor[:, at] = all_s[32:64, h, :]
    diagonal = lax.broadcasted_iota(jnp.int32, (64, LANES), 0) == lax.broadcasted_iota(
        jnp.int32, (64, LANES), 1
    )
    row = jnp.sum(jnp.where(diagonal, all_s[:, 2, :], 0.0), axis=0, keepdims=True)
    grad_bias[...] = row[:, 0:64]


def unpack(everyone):
    return pl.pallas_call(
        unpack_kernel,
        out_shape=[struct((32, 256), F32)] * 2 + [struct((1, 64), F32)],
        in_specs=[ANY],
        out_specs=[VMEM] * 3,
        scratch_shapes=[pltpu.VMEM(everyone.shape, F32), pltpu.SemaphoreType.DMA(())],
        compiler_params=params(),
        cost_estimate=cost(1e6, 1 << 18),
        name="unpack",
    )(everyone)


def exchange(pieces, sign):
    got = [pieces[0]]
    for s in range(1, 4):
        got.append(lax.ppermute(pieces[s], "feat", [(q, (q + sign * s) % 4) for q in range(4)]))
    return got


def per_device(
    quantized,
    node_scale,
    send_rows,
    send_count,
    tile_cols,
    edge_tiles,
    self_weight,
    neighbor_weight,
    hidden_bias,
    upstream,
):
    feat = lax.axis_index("feat").astype(jnp.int32)
    me = feat.reshape(1)
    cols = tile_cols[0]

    feat_tiles, wire, idx, *blocks = gather(
        quantized,
        node_scale.reshape(1, -1),
        send_rows,
        send_count,
        upstream,
        self_weight,
        neighbor_weight,
        hidden_bias.reshape(1, -1),
    )
    halo = lax.all_to_all(wire, "dom", split_axis=0, concat_axis=0, tiled=True)
    pieces = exchange(blocks, 1)
    mask, degree = masks(edge_tiles)

    others, joined, chunk, degree = aggregate(me, cols, feat_tiles, halo, degree, mask)
    aggs = exchange([aggregate_own(me, cols, joined, chunk, degree), *others], 1)
    backs, hiddens, sums = dense(me, pieces, aggs, degree)
    backs = exchange(backs, -1)
    begun = spread_own(me, cols, backs[0], chunk)
    local, back = spread(me, cols, begun, mask, backs)
    returned = lax.all_to_all(back, "dom", split_axis=0, concat_axis=0, tiled=True)
    local, hiddens, sums = lax.optimization_barrier((local, hiddens, sums))

    hidden = place(me, exchange(hiddens, -1))
    sums = exchange(sums, -1)
    everyone = lax.all_to_all(
        final_part(returned), "dom", split_axis=0, concat_axis=0, tiled=True
    )
    grad_features = scatter(me, idx, returned, local, sums)
    grad_self, grad_neighbor, grad_bias = unpack(everyone)
    return hidden, grad_features, grad_self, grad_neighbor, grad_bias.reshape(-1)


def solution(mesh):
    return jax.shard_map(
        per_device,
        mesh=mesh,
        in_specs=(
            P("feat", "dom"),
            P("dom"),
            P("dom", None, None),
            P("dom", None),
            P("dom", None, None),
            P("dom", None, None, None),
            P("feat", None),
            P("feat", None),
            P("feat"),
            P("feat", "dom"),
        ),
        out_specs=(P("feat", "dom"), P("feat", "dom"), P("feat", None), P("feat", None), P("feat")),
        check_vma=False,
    )
```

```python
import functools

import jax
import jax.numpy as jnp
from jax import lax
from jax.experimental import pallas as pl
from jax.experimental.pallas import tpu as pltpu
from jax.sharding import PartitionSpec as P

BF = jnp.bfloat16
F32 = jnp.float32
VMEM = pl.BlockSpec(memory_space=pltpu.VMEM)
ANY = pl.BlockSpec(memory_space=pl.ANY)
SMEM = pl.BlockSpec(memory_space=pltpu.SMEM)
LANES = 128
GROUP = 4


def params(mib=40):
    return pltpu.CompilerParams(vmem_limit_bytes=mib << 20)


def cost(flops, nbytes):
    return pl.CostEstimate(flops=int(flops), bytes_accessed=int(nbytes), transcendentals=0)


def low_half(shape):
    return lax.broadcasted_iota(jnp.int32, shape, len(shape) - 1) < LANES // 2


def split_rest(tile):
    half = tile.shape[0] // 2
    a, b = tile[:half], tile[half:]
    low = low_half(a.shape)
    even = jnp.where(low, a, pltpu.roll(b, LANES // 2, 1))
    odd = jnp.where(low, pltpu.roll(a, LANES // 2, 1), b)
    return even, odd


def join_rest(even, odd):
    low = low_half(even.shape)
    a = jnp.where(low, even, pltpu.roll(odd, LANES // 2, 1))
    b = jnp.where(low, pltpu.roll(even, LANES // 2, 1), odd)
    return jnp.concatenate([a, b], axis=0)


def one_hot_rows(lo, count):
    rows = lax.broadcasted_iota(jnp.int32, (count, lo.shape[1]), 0)
    return jnp.where(rows == lo, 1.0, 0.0).astype(BF)


class Copies:
    def __init__(self, src, dst, sems, first, parts):
        size = dst.shape[0] // parts
        self.parts = [
            pltpu.make_async_copy(
                src.at[pl.ds(n * size, size)], dst.at[pl.ds(n * size, size)], sems.at[first + n]
            )
            for n in range(parts)
        ]
        for part in self.parts:
            part.start()

    def wait(self):
        for part in self.parts:
            part.wait()


def turn(me, s):
    return lax.rem(me + 4 - s, 4)


def struct(shape, dtype):
    return jax.ShapeDtypeStruct(shape, dtype)


DEGREE_ROWS = 53248
LOCAL_TILES = 1664


FOLD_IN = 256
FOLD_OUT = 512


def gather_kernel(
    quantized, scale, rows, counts, upstream, self_w, neighbor_w, bias,
    tiles_out, wire_out, idx_out, b0, b1, b2, b3,
    q_s, s_s, r_s, c_s, sw_s, nw_s, bias_s, rest_s, folded, feat_tiles, wire, idx, block_s, sems,
):
    pairs = [(scale, s_s), (rows, r_s), (counts, c_s)]
    pairs += [(self_w, sw_s), (neighbor_w, nw_s), (bias, bias_s)]
    for n in range(4):
        at = pl.ds(n * 2048, 2048)
        pairs.append((quantized.at[:, at], q_s.at[:, at]))
    copies = [pltpu.make_async_copy(src, dst, sems.at[n]) for n, (src, dst) in enumerate(pairs)]
    for copy in copies:
        copy.start()
    for copy in copies:
        copy.wait()
    me = lax.axis_index("feat").astype(jnp.int32)
    odd = lax.rem(lax.axis_index("dom").astype(jnp.int32), 2)
    ups = []
    for s in range(4):
        at = pl.ds(pl.multiple_of(lax.rem(me + s, 4) * 2048, 2048), 2048)
        dst = block_s.at[s, pl.ds(32, 64)]
        ups.append(pltpu.make_async_copy(upstream.at[:, at], dst, sems.at[17 + s]))
        ups[s].start()
    feature_count, node_count = q_s.shape
    fold = node_count // FOLD_IN
    for c in range(fold):
        at = pl.ds(c * FOLD_IN, FOLD_IN)
        part = (q_s[:, at].astype(F32) * s_s[:, at]).astype(BF)
        folded[c * feature_count : (c + 1) * feature_count, :] = part
        for t in range(FOLD_IN // LANES):
            feat_tiles[c * (FOLD_IN // LANES) + t] = part[:, t * LANES : (t + 1) * LANES]

    peers = r_s.shape[1]
    spread_counts = jnp.broadcast_to(c_s[...], (peers, peers))
    diagonal = lax.broadcasted_iota(jnp.int32, (peers, peers), 0) == lax.broadcasted_iota(
        jnp.int32, (peers, peers), 1
    )
    limit = jnp.sum(jnp.where(diagonal, spread_counts, 0), axis=1, keepdims=True)
    lane = lax.broadcasted_iota(jnp.int32, (peers, LANES), 1)
    first = jnp.where(lane < limit, r_s[0, :, 0:LANES], -1)
    last = jnp.concatenate(
        [r_s[0, :, LANES : LANES + 64], jnp.full((peers, 64), -1, jnp.int32)], axis=1
    )
    last = jnp.where(lane + LANES < limit, last, -1)
    low = lane < 64
    moved = jnp.where(low, pltpu.roll(first, 64, 1), pltpu.roll(last, 64, 1))
    is_odd = jnp.full((peers, LANES), odd, jnp.int32) == 1
    idx[0:peers, :] = jnp.where(is_odd, moved, first)
    rest_s[...] = jnp.where(is_odd, first, last)
    even_rows = rest_s[pl.ds(0, peers // 2, stride=2), :]
    odd_rows = rest_s[pl.ds(1, peers // 2, stride=2), :]
    idx[peers : peers + peers // 2, :] = jnp.where(
        low[0 : peers // 2], even_rows, pltpu.roll(odd_rows, 64, 1)
    )

    per_block = node_count // 4 // LANES
    for s in range(4):
        begin = lax.rem(me + s, 4) * per_block
        for t in range(per_block):
            block_s[s, 0:32, t * LANES : (t + 1) * LANES] = feat_tiles[begin + t]
    whole_bias = jnp.broadcast_to(bias_s[...], (32, 64))
    for s in range(4):
        block_s[s, 96:128, 512:] = jnp.zeros((32, 1536), BF)
        block_s[s, 96:128, 0:256] = sw_s[...]
        block_s[s, 96:128, 256:512] = nw_s[...]
        left = whole_bias
        for n in range(3):
            part = left.astype(BF)
            block_s[s, 96:128, 512 + n * LANES : 576 + n * LANES] = part
            left = left - part.astype(F32)
    pairs = [(feat_tiles, tiles_out), (idx, idx_out)]
    for s, block in enumerate((b0, b1, b2, b3)):
        pairs.append((block_s.at[s], block))
    for copy in ups:
        copy.wait()
    sends = [
        pltpu.make_async_copy(src, dst, sems.at[21 + n]) for n, (src, dst) in enumerate(pairs)
    ]
    for send in sends:
        send.start()

    def pick(base):
        row = jnp.concatenate([idx[pl.ds(base + t, 1), :] for t in range(16)], axis=1)
        hi, lo = row >> 8, row & (FOLD_IN - 1)
        out = jnp.dot(folded[...], one_hot_rows(lo, FOLD_IN), preferred_element_type=F32)
        total = jnp.zeros((feature_count, row.shape[1]), F32)
        for c in range(fold):
            total = total + jnp.where(hi == c, out[c * feature_count : (c + 1) * feature_count], 0.0)
        return [total[:, t * LANES : (t + 1) * LANES] for t in range(16)]

    @pl.loop(0, 4, unroll=2)
    def _(g):
        tiles = pick(g * 16)
        for t in range(16):
            wire[g * 16 + t, 0:feature_count, :] = tiles[t].astype(BF)

    @pl.loop(0, 2, unroll=2)
    def _(g):
        tiles = pick(64 + g * 16)
        for t in range(16):
            even, odd_part = split_rest(tiles[t])
            wire[(g * 16 + t) * 2, feature_count:48, :] = even.astype(BF)
            wire[(g * 16 + t) * 2 + 1, feature_count:48, :] = odd_part.astype(BF)
        at = pl.ds(g * 32, 32)
        pltpu.make_async_copy(wire.at[at], wire_out.at[at], sems.at[13 + g]).start()

    for send in sends:
        send.wait()
    for g in range(2):
        at = pl.ds(g * 32, 32)
        pltpu.make_async_copy(wire.at[at], wire_out.at[at], sems.at[13 + g]).wait()


def gather(quantized, scale, rows, counts, *early):
    features, nodes = quantized.shape
    return pl.pallas_call(
        gather_kernel,
        out_shape=[
            struct((nodes // LANES, features, LANES), BF),
            struct((64, 48, LANES), BF),
            struct((96, LANES), jnp.int32),
        ]
        + [struct((128, nodes // 4), BF)] * 4,
        in_specs=[ANY] * 8,
        out_specs=[ANY] * 7,
        scratch_shapes=[
            pltpu.VMEM(quantized.shape, BF),
            pltpu.VMEM(scale.shape, F32),
            pltpu.VMEM(rows.shape, jnp.int32),
            pltpu.VMEM(counts.shape, jnp.int32),
            pltpu.VMEM((32, 256), BF),
            pltpu.VMEM((32, 256), BF),
            pltpu.VMEM((1, 64), F32),
            pltpu.VMEM((64, LANES), jnp.int32),
            pltpu.VMEM((features * nodes // FOLD_IN, FOLD_IN), BF),
            pltpu.VMEM((nodes // LANES, features, LANES), BF),
            pltpu.VMEM((64, 48, LANES), BF),
            pltpu.VMEM((96, LANES), jnp.int32),
            pltpu.VMEM((4, 128, nodes // 4), BF),
            pltpu.SemaphoreType.DMA((27,)),
        ],
        compiler_params=params(60),
        cost_estimate=cost(6.4e9, 4 << 20),
        name="gather_rows",
    )(quantized, scale, rows, counts, *early)


def mask_kernel(edges, mask, degree_out, edges_s, mask_s, degree, in_sems, out_sems):
    steps = edges.shape[0] // GROUP
    ones = jnp.ones((8, LANES), BF)
    loads = []
    stores = []
    for i in range(steps):
        at = pl.ds(i * GROUP, GROUP)
        loads.append(pltpu.make_async_copy(edges.at[at], edges_s.at[at], in_sems.at[i]))
        stores.append(pltpu.make_async_copy(mask_s.at[at], mask.at[at], out_sems.at[i]))
        loads[i].start()
    for i in range(steps):
        loads[i].wait()
        for r in range(i * GROUP, (i + 1) * GROUP):
            whole = edges_s[r]
            mask_s[r] = whole.astype(F32).astype(BF)
            total = (whole[0] + whole[1] + whole[2] + whole[3]).astype(F32).astype(BF)
            degree[r] = lax.dot_general(
                ones, total, (((1,), (1,)), ((), ())), preferred_element_type=F32
            )[0:1]
        stores[i].start()
    stores.append(
        pltpu.make_async_copy(degree, degree_out.at[pl.ds(0, degree.shape[0])], in_sems.at[0])
    )
    stores[-1].start()
    for store in stores:
        store.wait()


def masks(edges):
    tiles = edges.shape[0]
    length = 4 * tiles
    return pl.pallas_call(
        mask_kernel,
        out_shape=[struct((length,) + edges.shape[1:], BF), struct((DEGREE_ROWS, 1, LANES), F32)],
        in_specs=[ANY],
        out_specs=[ANY, ANY],
        scratch_shapes=[
            pltpu.VMEM(edges.shape, jnp.int32),
            pltpu.VMEM(edges.shape, BF),
            pltpu.VMEM((tiles, 1, LANES), F32),
            pltpu.SemaphoreType.DMA((tiles // GROUP,)),
            pltpu.SemaphoreType.DMA((tiles // GROUP,)),
        ],
        compiler_params=params(58),
        cost_estimate=cost(1e9, 24 << 20),
        name="mask_degree",
    )(edges)


QUARTER = 16


PARTS = 4


def fetch(me, shift, mask, chunk, sems, first=0):
    begin = lax.rem(me[0] + shift, 4) * QUARTER
    return Copies(mask.at[pl.ds(begin, QUARTER)], chunk, sems, first, PARTS)


CHUNK = struct((QUARTER, 4, LANES, LANES), BF)


def aggregate_tiles(begin, cols, joined, chunk, degree, out):
    totals = []
    for t in range(QUARTER):
        row = begin + t
        picked = jnp.concatenate([joined[cols[row, k]] for k in range(4)], axis=1)
        flat = jnp.concatenate([chunk[t, k] for k in range(4)], axis=1)
        totals.append(
            lax.dot_general(picked, flat, (((1,), (1,)), ((), ())), preferred_element_type=F32)
        )
    for t in range(QUARTER):
        row = begin + t
        out[:, t * LANES : (t + 1) * LANES] = (
            (totals[t] + joined[row].astype(F32)) / (degree[row] + 1.0)
        ).astype(BF)


ORDER = (2, 1, 3)


def aggregate_kernel(me, cols, feat_tiles, wire, degree_in, mask, *refs):
    outs, (joined, own_chunk, degree, chunks, sems) = refs[0:3], refs[3:]
    counts = Copies(degree_in.at[pl.ds(0, 64)], degree, sems, 3, 1)
    local = 64
    own = Copies(feat_tiles, joined.at[pl.ds(0, local)], sems, 2, 1)
    tiles = [
        fetch(me, shift, mask, chunks.at[n], sems, 8 + PARTS * n) for n, shift in enumerate(ORDER)
    ]

    @pl.loop(0, 32, unroll=8)
    def _(q):
        even, odd = wire[2 * q], wire[2 * q + 1]
        joined[local + 3 * q] = even[0:32]
        joined[local + 3 * q + 2] = odd[0:32]
        joined[local + 3 * q + 1] = join_rest(even[32:48].astype(F32), odd[32:48].astype(F32)).astype(BF)

    own.wait()
    counts.wait()
    for n, shift in enumerate(ORDER):
        tiles[n].wait()
        begin = lax.rem(me[0] + shift, 4) * QUARTER
        if n == 1:
            later = fetch(me, 0, mask, own_chunk, sems, 8 + PARTS * 3)
        aggregate_tiles(begin, cols, joined, chunks.at[n], degree, outs[shift - 1])
    later.wait()


def aggregate(me, cols, feat_tiles, wire, degree, mask):
    rows = feat_tiles.shape[1]
    got = pl.pallas_call(
        aggregate_kernel,
        out_shape=[struct((rows, 2048), BF)] * 3 + [struct((160, rows, LANES), BF), CHUNK]
        + [struct((64, 1, LANES), F32)],
        in_specs=[SMEM, SMEM, ANY, VMEM, ANY, ANY],
        out_specs=[VMEM] * 6,
        scratch_shapes=[
            pltpu.VMEM((3,) + CHUNK.shape, BF),
            pltpu.SemaphoreType.DMA((8 + PARTS * 4,)),
        ],
        compiler_params=params(),
        cost_estimate=cost(3e9, 12 << 20),
        name="aggregate",
    )(me, cols, feat_tiles, wire, degree, mask)
    return got[0:3], got[3], got[4], got[5]


def aggregate_own_kernel(me, cols, joined, chunk, degree, out):
    aggregate_tiles(me[0] * QUARTER, cols, joined, chunk, degree, out)


def aggregate_own(me, cols, joined, chunk, degree):
    return pl.pallas_call(
        aggregate_own_kernel,
        out_shape=struct((joined.shape[1], 2048), BF),
        in_specs=[SMEM, SMEM, VMEM, VMEM, VMEM],
        out_specs=VMEM,
        compiler_params=params(),
        cost_estimate=cost(1e9, 4 << 20),
        name="aggregate_own",
    )(me, cols, joined, chunk, degree)


def dense_kernel(me_ref, *refs):
    pieces, aggs, degree = refs[0:4], refs[4:8], refs[8]
    backs, hiddens, sums = refs[9:13], refs[13:17], refs[17:21]
    stage, agg, slope, hid_s, back_s, sum_s, sems = refs[21:]
    me = me_ref[0]
    both = (((1,), (1,)), ((), ()))
    nodes = slope.shape[1]
    copies = []
    for s in range(4):
        at = pl.ds(pl.multiple_of(turn(me, s) * 32, 32), 32)
        copies.append(pltpu.make_async_copy(aggs[s], agg.at[at, :], sems.at[s]))
        copies.append(pltpu.make_async_copy(pieces[s], stage.at[turn(me, s)], sems.at[4 + s]))
    for copy in copies:
        copy.start()
    for copy in copies:
        copy.wait()

    def joint(first, last, at):
        return jnp.concatenate([stage[b, first:last, at] for b in range(4)], axis=0)

    self_w = joint(96, 128, slice(0, 256))
    neighbor_w = joint(96, 128, slice(256, 512))
    self_t = self_w.astype(F32).T.astype(BF)
    neighbor_t = neighbor_w.astype(F32).T.astype(BF)
    diagonal = lax.broadcasted_iota(jnp.int32, (64, 64), 0) == lax.broadcasted_iota(
        jnp.int32, (64, 64), 1
    )
    columns = []
    for b in range(4):
        row = sum(
            stage[b, 96:112, 512 + n * LANES : 576 + n * LANES].astype(F32) for n in range(3)
        )[0:1]
        square = jnp.where(diagonal, jnp.broadcast_to(row, (64, 64)), 0.0)
        columns.append(jnp.sum(square, axis=1, keepdims=True))
    bias = jnp.concatenate(columns, axis=0)
    sends = []

    def send(pieces, whole, size, first):
        for s in range(4):
            if whole.shape[0] == 4:
                src = whole.at[turn(me, s)]
            else:
                src = whole.at[pl.ds(pl.multiple_of(turn(me, s) * size, size), size), :]
            sends.append(pltpu.make_async_copy(src, pieces[s], sems.at[first + s]))
            sends[-1].start()

    for n in range(4):
        at = slice(n * 512, (n + 1) * 512)
        preact = (
            jnp.dot(self_t, joint(0, 32, at), preferred_element_type=F32)
            + jnp.dot(neighbor_t, agg[:, at], preferred_element_type=F32)
            + bias
        )
        sig = jax.nn.sigmoid(preact)
        hid_s[:, at] = (preact * sig).astype(BF)
        part = (
            joint(32, 96, at).astype(F32) * sig * (1.0 + preact * (1.0 - sig))
        ).astype(BF)
        slope[:, at] = part
        below = jnp.concatenate([degree[me * 16 + n * 4 + t] for t in range(4)], axis=1) + 1.0
        whole = jnp.dot(neighbor_w, part, preferred_element_type=F32) / below
        for b in range(4):
            back_s[b, 0:32, at] = whole[b * 32 : (b + 1) * 32].astype(BF)
        own = jnp.dot(self_w, part, preferred_element_type=F32)
        sum_s[:, at] = (own + whole).astype(BF)
    send(hiddens, hid_s, 64, 12)
    send(sums, sum_s, 32, 16)
    all_nodes = slice(0, nodes)
    feat_grad = lax.dot_general(
        joint(0, 32, all_nodes), slope[...], both, preferred_element_type=F32
    )
    agg_grad = lax.dot_general(agg[...], slope[...], both, preferred_element_type=F32)
    bias_grad = lax.dot_general(
        jnp.ones((8, nodes), BF), slope[...], both, preferred_element_type=F32
    )
    bias_row = bias_grad[0:1]
    high = bias_row.astype(BF).astype(F32)
    for b in range(4):
        for n, grad in enumerate((feat_grad, agg_grad)):
            for h in range(4):
                first = b * 32 + h * 8
                at = slice((4 * n + h) * 256, (4 * n + h + 1) * 256)
                back_s[b, 32:40, at] = grad[first : first + 8].astype(BF)
        own = slice(b * 64, (b + 1) * 64)
        both_parts = jnp.concatenate([high[:, own], (bias_row - high)[:, own]], axis=1)
        back_s[b, 0:32, nodes:] = jnp.zeros((32, LANES), BF)
        back_s[b, 32:40, nodes:] = jnp.broadcast_to(both_parts, (8, LANES)).astype(BF)
    send(backs, back_s, 40, 8)
    for copy in sends:
        copy.wait()


def dense(me, pieces, aggs, degree):
    nodes = aggs[0].shape[1]
    got = pl.pallas_call(
        dense_kernel,
        out_shape=[struct((40, nodes + LANES), BF)] * 4
        + [struct((64, nodes), BF)] * 4
        + [struct((32, nodes), BF)] * 4,
        in_specs=[SMEM] + [ANY] * 8 + [VMEM],
        out_specs=[ANY] * 12,
        scratch_shapes=[
            pltpu.VMEM((4, 128, nodes), BF),
            pltpu.VMEM((128, nodes), BF),
            pltpu.VMEM((256, nodes), BF),
            pltpu.VMEM((256, nodes), BF),
            pltpu.VMEM((4, 40, nodes + LANES), BF),
            pltpu.VMEM((128, nodes), BF),
            pltpu.SemaphoreType.DMA((20,)),
        ],
        compiler_params=params(56),
        cost_estimate=cost(1e9, 5 << 20),
        name="dense",
    )(me, *pieces, *aggs, degree)
    return got[0:4], got[4:8], got[8:12]


def pack_grads(grad, row, pack_s):
    diagonal = lax.broadcasted_iota(jnp.int32, (64, 64), 0) == lax.broadcasted_iota(
        jnp.int32, (64, 64), 1
    )
    column = jnp.sum(
        jnp.where(diagonal, jnp.broadcast_to(row, (64, 64)), 0.0), axis=1, keepdims=True
    )
    values = [grad[:, 0:LANES], grad[:, LANES:], jnp.broadcast_to(column, (64, LANES))]
    for n, value in enumerate(values):
        high = value.astype(BF).astype(F32)
        pack_s[:, n, :] = high
        pack_s[:, n + 3, :] = value - high
    for n in (6, 7):
        pack_s[:, n, :] = jnp.zeros((64, LANES), F32)


def spread_tiles(begin, cols, mean, chunk, total):
    for half in range(2):
        parts = []
        for t in range(half * 8, half * 8 + 8):
            flat = jnp.concatenate([chunk[t, k] for k in range(4)], axis=1)
            parts.append(
                jnp.dot(mean[0:32, t * LANES : (t + 1) * LANES], flat, preferred_element_type=F32)
            )
        for t in range(8):
            for k in range(4):
                at = cols[begin + half * 8 + t, k]
                total[at] = total[at] + parts[t][:, k * LANES : (k + 1) * LANES]


def spread_own_kernel(me, cols, mean, chunk, mask, total, *refs):
    later, sems = refs[0:3], refs[3]
    tiles = [fetch(me, s, mask, later[s - 1], sems, PARTS * (s - 1)) for s in (1, 2, 3)]
    total[...] = jnp.zeros(total.shape, F32)
    spread_tiles(me[0] * QUARTER, cols, mean, chunk, total)
    for copy in tiles:
        copy.wait()


def spread_own(me, cols, mean, chunk, mask):
    got = pl.pallas_call(
        spread_own_kernel,
        out_shape=[struct((160, 32, LANES), F32)] + [CHUNK] * 3,
        in_specs=[SMEM, SMEM, VMEM, VMEM, ANY],
        out_specs=[VMEM] * 4,
        scratch_shapes=[pltpu.SemaphoreType.DMA((3 * PARTS,))],
        compiler_params=params(),
        cost_estimate=cost(1e9, 8 << 20),
        name="spread_own",
    )(me, cols, mean, chunk, mask)
    return got[0], got[1:4]


def spread_kernel(me, cols, begun, *refs):
    chunks, backs, (local, wire_out), refs = refs[0:3], refs[3:7], refs[7:9], refs[9:]
    total, back_s, pack_s, wire, sems = refs
    pieces = []
    for s in range(4):
        pieces.append(pltpu.make_async_copy(backs[s], back_s.at[s], sems.at[s]))
        pieces[-1].start()
    total[...] = begun[...]
    for s in (1, 2, 3):
        begin = lax.rem(me[0] + s, 4) * QUARTER
        pieces[s].wait()
        spread_tiles(begin, cols, back_s.at[s], chunks[s - 1], total)
    own = Copies(total.at[pl.ds(0, 64)], local.at[pl.ds(0, 64)], sems, 8, 2)
    pieces[0].wait()
    grads = sum(back_s[s, 32:40, :].astype(F32) for s in range(4))
    grad = jnp.concatenate([grads[:, n * 256 : (n + 1) * 256] for n in range(8)], axis=0)
    pack_grads(grad, grads[0:1, 2048:2112] + grads[0:1, 2112:2176], pack_s)
    wire[:, 48:56, :] = pack_s[...].astype(BF)

    @pl.loop(0, 32, unroll=8)
    def _(q):
        wire[2 * q, 0:32, :] = total[64 + 3 * q].astype(BF)
        wire[2 * q + 1, 0:32, :] = total[64 + 3 * q + 2].astype(BF)
        even, odd = split_rest(total[64 + 3 * q + 1])
        wire[2 * q, 32:48, :] = even.astype(BF)
        wire[2 * q + 1, 32:48, :] = odd.astype(BF)

    leaving = Copies(wire, wire_out, sems, 4, 4)
    own.wait()
    leaving.wait()


def spread(me, cols, begun, chunks, backs):
    _, rows, _ = begun.shape
    return pl.pallas_call(
        spread_kernel,
        out_shape=[struct((LOCAL_TILES, rows, LANES), F32), struct((64, 56, LANES), BF)],
        in_specs=[SMEM, SMEM] + [VMEM] * 4 + [ANY] * 4,
        out_specs=[ANY] * 2,
        scratch_shapes=[
            pltpu.VMEM(begun.shape, F32),
            pltpu.VMEM((4,) + backs[0].shape, BF),
            pltpu.VMEM((64, 8, LANES), F32),
            pltpu.VMEM((64, 56, LANES), BF),
            pltpu.SemaphoreType.DMA((10,)),
        ],
        compiler_params=params(),
        cost_estimate=cost(3e9, 12 << 20),
        name="spread",
    )(me, cols, begun, *chunks, *backs)


def scatter_kernel(me_ref, idx, wire, local, *refs):
    sums, out, sum_s, ret, acc, idx_s, own_s, out_s, sems = refs[0:4], *refs[4:]
    me = me_ref[0]
    index = Copies(idx, idx_s, sems, 0, 1)
    later = [Copies(local.at[pl.ds(0, 64)], own_s, sems, 5, 2)]
    for s in range(4):
        later.append(Copies(sums[s], sum_s.at[lax.rem(me + s, 4)], sems, 9 + s, 1))
    nodes = out.shape[1]
    fold = nodes // FOLD_OUT
    acc[...] = jnp.zeros(acc.shape, F32)
    index.wait()

    @pl.loop(0, 32, unroll=8)
    def _(q):
        even, odd = wire[2 * q], wire[2 * q + 1]
        ret[2 * q] = even[0:32].astype(F32)
        ret[2 * q + 1] = odd[0:32].astype(F32)
        ret[64 + q] = join_rest(even[32:48].astype(F32), odd[32:48].astype(F32))

    @pl.loop(0, 6, unroll=2)
    def _(g):
        row = jnp.concatenate([idx_s[pl.ds(g * 16 + t, 1), :] for t in range(16)], axis=1)
        hi, lo = row >> 9, row & (FOLD_OUT - 1)
        value = jnp.concatenate([ret[g * 16 + t] for t in range(16)], axis=1)
        folded = jnp.concatenate(
            [jnp.where(hi == c, value, 0.0).astype(BF) for c in range(fold)], axis=0
        )
        acc[...] += lax.dot_general(
            folded, one_hot_rows(lo, FOLD_OUT), (((1,), (1,)), ((), ())), preferred_element_type=F32
        )

    for copy in later:
        copy.wait()
    per = FOLD_OUT // LANES
    sends = []
    for quarter in range(4):
        for inner in range(fold // 4):
            c = quarter * (fold // 4) + inner
            inside = inner * FOLD_OUT
            own = jnp.concatenate([own_s[c * per + t] for t in range(per)], axis=1)
            extra = sum_s[quarter, :, inside : inside + FOLD_OUT].astype(F32)
            out_s[:, c * FOLD_OUT : (c + 1) * FOLD_OUT] = acc[c * 32 : (c + 1) * 32, :] + own + extra
        at = pl.ds(quarter * 2048, 2048)
        sends.append(pltpu.make_async_copy(out_s.at[:, at], out.at[:, at], sems.at[13 + quarter]))
        sends[-1].start()
    for send in sends:
        send.wait()


def scatter(me, idx, wire, local, sums):
    rows = sums[0].shape[0]
    return pl.pallas_call(
        scatter_kernel,
        out_shape=struct((rows, 8192), F32),
        in_specs=[SMEM, ANY, VMEM] + [ANY] * 5,
        out_specs=ANY,
        scratch_shapes=[
            pltpu.VMEM((4, rows, 2048), BF),
            pltpu.VMEM((96, rows, LANES), F32),
            pltpu.VMEM((rows * 8192 // FOLD_OUT, FOLD_OUT), F32),
            pltpu.VMEM((96, LANES), jnp.int32),
            pltpu.VMEM((64, rows, LANES), F32),
            pltpu.VMEM((rows, 8192), F32),
            pltpu.SemaphoreType.DMA((17,)),
        ],
        compiler_params=params(),
        cost_estimate=cost(6.4e9, 5 << 20),
        name="scatter_rows",
    )(me, idx, wire, local, *sums)


def place_kernel(me_ref, a, b, c, d, out):
    for s, piece in enumerate((a, b, c, d)):
        at = pl.ds(pl.multiple_of(lax.rem(me_ref[0] + s, 4) * 2048, 2048), 2048)
        out[:, at] = piece[...]


def place(me, pieces):
    rows = pieces[0].shape[0]
    return pl.pallas_call(
        place_kernel,
        out_shape=struct((rows, 8192), BF),
        in_specs=[SMEM] + [VMEM] * 4,
        out_specs=VMEM,
        compiler_params=params(),
        cost_estimate=cost(1e6, 2 << 20),
        name="place",
    )(me, *pieces)


def final_kernel(returned, final):
    total = jnp.sum(returned[:, 48:56, :].astype(F32), axis=0)
    final[...] = jnp.broadcast_to((total[0:4] + total[3:7])[None], final.shape)


def final_part(returned):
    return pl.pallas_call(
        final_kernel,
        out_shape=struct((64, 4, LANES), F32),
        in_specs=[VMEM],
        out_specs=VMEM,
        compiler_params=params(),
        cost_estimate=cost(1e6, 1 << 18),
        name="final_part",
    )(returned)


def unpack_kernel(everyone, grad_self, grad_neighbor, grad_bias, all_s, sem):
    copy = pltpu.make_async_copy(everyone, all_s, sem)
    copy.start()
    copy.wait()
    for h in range(2):
        at = pl.ds(h * LANES, LANES)
        grad_self[:, at] = all_s[0:32, h, :]
        grad_neighbor[:, at] = all_s[32:64, h, :]
    diagonal = lax.broadcasted_iota(jnp.int32, (64, LANES), 0) == lax.broadcasted_iota(
        jnp.int32, (64, LANES), 1
    )
    row = jnp.sum(jnp.where(diagonal, all_s[:, 2, :], 0.0), axis=0, keepdims=True)
    grad_bias[...] = row[:, 0:64]


def unpack(everyone):
    return pl.pallas_call(
        unpack_kernel,
        out_shape=[struct((32, 256), F32)] * 2 + [struct((1, 64), F32)],
        in_specs=[ANY],
        out_specs=[VMEM] * 3,
        scratch_shapes=[pltpu.VMEM(everyone.shape, F32), pltpu.SemaphoreType.DMA(())],
        compiler_params=params(),
        cost_estimate=cost(1e6, 1 << 18),
        name="unpack",
    )(everyone)


def exchange(pieces, sign):
    got = [pieces[0]]
    for s in range(1, 4):
        got.append(lax.ppermute(pieces[s], "feat", [(q, (q + sign * s) % 4) for q in range(4)]))
    return got


def per_device(
    quantized,
    node_scale,
    send_rows,
    send_count,
    tile_cols,
    edge_tiles,
    self_weight,
    neighbor_weight,
    hidden_bias,
    upstream,
):
    feat = lax.axis_index("feat").astype(jnp.int32)
    me = feat.reshape(1)
    cols = tile_cols[0]

    feat_tiles, wire, idx, *blocks = gather(
        quantized,
        node_scale.reshape(1, -1),
        send_rows,
        send_count,
        upstream,
        self_weight,
        neighbor_weight,
        hidden_bias.reshape(1, -1),
    )
    halo = lax.all_to_all(wire, "dom", split_axis=0, concat_axis=0, tiled=True)
    pieces = exchange(blocks, 1)
    mask, degree = masks(edge_tiles)

    others, joined, chunk, degree = aggregate(me, cols, feat_tiles, halo, degree, mask)
    aggs = exchange([aggregate_own(me, cols, joined, chunk, degree), *others], 1)
    backs, hiddens, sums = dense(me, pieces, aggs, degree)
    backs = exchange(backs, -1)
    begun, chunks = spread_own(me, cols, backs[0], chunk, mask)
    local, back = spread(me, cols, begun, chunks, backs)
    returned = lax.all_to_all(back, "dom", split_axis=0, concat_axis=0, tiled=True)
    local, hiddens, sums = lax.optimization_barrier((local, hiddens, sums))

    hidden = place(me, exchange(hiddens, -1))
    sums = exchange(sums, -1)
    everyone = lax.all_to_all(
        final_part(returned), "dom", split_axis=0, concat_axis=0, tiled=True
    )
    grad_features = scatter(me, idx, returned, local, sums)
    grad_self, grad_neighbor, grad_bias = unpack(everyone)
    return hidden, grad_features, grad_self, grad_neighbor, grad_bias.reshape(-1)


def solution(mesh):
    return jax.shard_map(
        per_device,
        mesh=mesh,
        in_specs=(
            P("feat", "dom"),
            P("dom"),
            P("dom", None, None),
            P("dom", None),
            P("dom", None, None),
            P("dom", None, None, None),
            P("feat", None),
            P("feat", None),
            P("feat"),
            P("feat", "dom"),
        ),
        out_specs=(P("feat", "dom"), P("feat", "dom"), P("feat", None), P("feat", None), P("feat")),
        check_vma=False,
    )
```
